32 devices in a mesh: seq: 16 (over z, y, x), ch: 2 (over core).
Axes of the slice: x: 2, y: 2, z: 4, core: 2. Of those that a mesh axis runs over, the one named last changes fastest.
Arguments:
- q_proj: bfloat16 [2048, 4096], P('seq', 'ch'), may hold values from -16 to 16
- k_proj: bfloat16 [2048, 4096], P('seq', 'ch'), may hold values from -6 to 6
- v_proj: bfloat16 [2048, 4096], P('seq', 'ch'), may hold values from -6 to 6
- feat_filter: float32 [3, 3, 4096], P(None, None, 'ch'), may hold values from -3.5 to 3.5
- long_filter: float32 [2048, 4096], P('seq', 'ch'), may hold values from -0.125 to 0.125
- skip_bias: float32 [4096], P('ch'), may hold values from -4 to 4
- norm_gain: float32 [4096], P('ch'), may hold values from 0.1 to 1.9
Outputs:
- mixed_out: bfloat16 [2048, 4096], P('seq', 'ch')
- normed: bfloat16 [2048, 4096], P('seq', 'ch')
The draws below stay inside these ranges and needn't reach their ends.
All inputs are finite; a program needn't handle non-finite values.
Results may differ from the reference program's by a relative error of at most 0.015.
Values may be sent and summed in bfloat16 or wider, within the bound.
A program may use at most 64 MiB of HBM per device.

```python
import math
import jax
import jax.numpy as jnp
from jax import lax

D = 4096
FEAT = 3
SEQ = 2048


def draw_q_proj(key, part):
    ramp = 1.0 + 2.0 * jnp.arange(D, dtype=jnp.float32) / (D - 1)
    base = jax.random.truncated_normal(key, -4.0, 4.0, (SEQ, D), jnp.float32)
    return (base * ramp[None, :]).astype(jnp.bfloat16)


def steps_of(stream_key, shape, cuts, low, top_value):
    loudness, own = 1.0, jax.random.fold_in(stream_key, 6)
    for axis_at, parts in cuts:
        draws = jnp.exp(jax.random.uniform(jax.random.fold_in(own, axis_at), (parts,), jnp.float32, low / len(cuts), top_value / len(cuts)))
        loudness = loudness * jnp.repeat(draws, shape[axis_at] // parts).reshape([-1 if axis == axis_at else 1 for axis in range(len(shape))])
    return loudness


def normal_values(stream_key, dims, scale, limit, cuts=(), held_as=jnp.bfloat16):
    level = steps_of(stream_key, dims, cuts, -0.22, 0.18) if cuts else 1.0
    values = jax.random.normal(stream_key, dims, jnp.float32) * scale * level
    return jnp.minimum(jnp.maximum(values, -limit), limit).astype(held_as)


def setup_inputs(seed: int = 0) -> dict:
    key_list = jax.random.split(jax.random.key(seed), 8)
    q_proj = draw_q_proj(jax.random.fold_in(key_list[7], 71), 0)
    k_proj = normal_values(key_list[1], (SEQ, D), 1.0, 6.0, ((0, 16), (1, 2)))
    v_proj = normal_values(key_list[2], (SEQ, D), 1.0, 6.0, ((0, 16), (1, 2)))
    feat_filter = normal_values(key_list[3], (3, FEAT, D), FEAT ** -0.5, 3.5, ((2, 2),), jnp.float32)
    long_filter = normal_values(key_list[4], (SEQ, D), SEQ ** -0.5, 0.125, ((0, 16), (1, 2)), jnp.float32)
    skip_bias = normal_values(key_list[5], (D,), 1.0, 4.0, ((0, 2),), jnp.float32)
    norm_gain = jnp.clip(1.0 + 0.18 * jax.random.normal(key_list[6], (D,), jnp.float32), 0.1, 1.9)
    return {"q_proj": q_proj, "k_proj": k_proj, "v_proj": v_proj, "feat_filter": feat_filter, "long_filter": long_filter, "skip_bias": skip_bias, "norm_gain": norm_gain}


def block_layer(query, keyed, valued, short_taps, filt, bias):
    stacked = jnp.stack([query, keyed, valued]).astype(jnp.float32)
    length = stacked.shape[1]
    taps = short_taps.shape[1]
    padded = jnp.pad(stacked, ((0, 0), (taps - 1, 0), (0, 0)))
    featured = jnp.zeros(stacked.shape, jnp.float32)
    for offset in range(taps):
        featured = featured + short_taps[:, offset, None, :] * padded[:, taps - 1 - offset:taps - 1 - offset + length, :]
    gated = featured[1] * featured[2]
    total = 2 * length
    spectrum = jnp.fft.rfft(gated, n=total, axis=0) * jnp.fft.rfft(filt, n=total, axis=0)
    long_conv = jnp.fft.irfft(spectrum, n=total, axis=0)[:length]
    return featured[0] * (long_conv + bias * gated)

def reference(q_proj, k_proj, v_proj, feat_filter, long_filter, skip_bias, norm_gain):
    width = math.gcd(D, 512)
    count = D // width

    def split(array):
        return array.reshape(SEQ, count, width).transpose(1, 0, 2)
    filters = feat_filter.reshape(3, FEAT, count, width).transpose(2, 0, 1, 3)
    biases = skip_bias.reshape(count, width)

    def one_block(pieces):
        return block_layer(pieces[0], pieces[1], pieces[2], pieces[3], pieces[4], pieces[5])
    mixed = lax.map(one_block, (split(q_proj), split(k_proj), split(v_proj), filters, split(long_filter), biases))
    mixed = mixed.transpose(1, 0, 2).reshape(SEQ, D)
    squares = lax.optimization_barrier(jnp.sum(mixed * mixed, axis=1, keepdims=True))
    scale = lax.rsqrt(squares / D + 1e-05)
    return (mixed.astype(jnp.bfloat16), (mixed * scale * norm_gain).astype(jnp.bfloat16))
```

```python
import functools
import math

import jax
import jax.numpy as jnp
import numpy as np
from jax import lax
from jax.experimental import pallas as pl
from jax.experimental.pallas import tpu as pltpu
from jax.sharding import PartitionSpec as P

D = 4096
RADIX = 16
HALF = RADIX // 2
LANES = 128
MESH = pl.DeviceIdType.MESH


def dft_tables(seq):
    length = 2 * seq
    inner = length // RADIX
    tokens = np.arange(inner, dtype=np.int64)

    def waves(freq):
        angle = (freq[:, None] * tokens[None, :] % length) * (2.0 * math.pi / length)
        return np.cos(angle), np.sin(angle)

    full = []
    for k1 in range(1, HALF):
        c, s = waves(k1 + RADIX * np.arange(inner, dtype=np.int64))
        full.append(np.block([[c, s], [-s, c]]))
    real = []
    for k1 in (0, HALF):
        c, s = waves(k1 + RADIX * np.arange(inner // 2, dtype=np.int64))
        table = np.concatenate([c, -s])
        if k1 == 0:
            table[inner // 2] = np.cos(math.pi * tokens)
        real.append(table)

    def split(table):
        high = table.astype(jnp.bfloat16)
        low = (table - high.astype(np.float64)).astype(jnp.bfloat16)
        return np.concatenate([high, low], axis=-1)

    full, real = np.stack(full), np.stack(real)
    turn = lambda a: np.swapaxes(a, 1, 2)
    return split(full), split(real), split(turn(full)), split(turn(real))


def turned(cr, ci, a):
    return (cr * a[0] - ci * a[1], cr * a[1] + ci * a[0])


def unit(power):
    angle = 2.0 * math.pi * power / RADIX
    return math.cos(angle), math.sin(angle)


def block_dft(x):
    s = math.sqrt(0.5)
    a = [x[n] + x[n + 4] for n in range(4)]
    b = [x[n] - x[n + 4] for n in range(4)]
    out = {}
    e, o = a[0] + a[2], a[1] + a[3]
    out[0], out[8] = e + o, e - o
    out[4] = (a[0] - a[2], a[3] - a[1])
    d, m = s * (b[1] - b[3]), s * (b[1] + b[3])
    out[2] = (b[0] + d, -b[2] - m)
    out[6] = (b[0] - d, b[2] - m)
    for first, sign in ((1, -1.0), (3, 1.0)):
        t = [(x[0], sign * x[4])]
        for n in range(1, 4):
            cr, ci = unit(-first * n)
            t.append(turned(cr, ci, (x[n], sign * x[n + 4])))
        er, ei = t[0][0] + t[2][0], t[0][1] + t[2][1]
        dr, di = t[0][0] - t[2][0], t[0][1] - t[2][1]
        fr, fi = t[1][0] + t[3][0], t[1][1] + t[3][1]
        gr, gi = t[1][0] - t[3][0], t[1][1] - t[3][1]
        out[first] = (er + fr, ei + fi)
        out[first + 4] = (dr + gi, di - gr)
    return out


def block_idft(u):
    s = math.sqrt(0.5)
    p, m = u[0] + u[8], u[0] - u[8]
    a = [p + u[4][0], m - u[4][1], p - u[4][0], m + u[4][1]]
    b = [
        u[2][0] + u[6][0],
        s * ((u[2][0] - u[2][1]) - (u[6][0] + u[6][1])),
        u[6][1] - u[2][1],
        s * ((u[6][0] - u[6][1]) - (u[2][0] + u[2][1])),
    ]
    out = [None] * HALF
    for n in range(4):
        low, high = a[n] + b[n], a[n] - b[n]
        for first, sign in ((1, -1.0), (3, 1.0)):
            v, w = u[first], u[first + 4]
            if n == 0:
                v = (v[0] + w[0], v[1] + w[1])
            elif n == 1:
                v = (v[0] - w[1], v[1] + w[0])
            elif n == 2:
                v = (v[0] - w[0], v[1] - w[1])
            else:
                v = (v[0] + w[1], v[1] - w[0])
            q = turned(*unit(first * n), v)
            low, high = low + q[0], high + sign * q[1]
        out[n], out[n + 4] = low, high
    return out


CHUNK = 32


def spread_blocks(inner, load, y_full, y_real):
    def step(i, carry):
        start = pl.multiple_of(i * CHUNK, CHUNK)
        rows = pl.ds(start, CHUNK)
        out = block_dft([load(n, start) for n in range(HALF)])
        y_real[0, rows, :] = out[0].astype(jnp.bfloat16)
        y_real[1, rows, :] = out[HALF].astype(jnp.bfloat16)
        lower = pl.ds(pl.multiple_of(inner + start, CHUNK), CHUNK)
        for k in range(1, HALF):
            y_full[k - 1, rows, :] = out[k][0].astype(jnp.bfloat16)
            y_full[k - 1, lower, :] = out[k][1].astype(jnp.bfloat16)
        return carry

    lax.fori_loop(0, inner // CHUNK, step, 0)


def both(table, values):
    half = table.shape[1] // 2
    first = jnp.dot(table[:, :half], values, preferred_element_type=jnp.float32)
    return first + jnp.dot(table[:, half:], values, preferred_element_type=jnp.float32)


def filter_spectrum(f_full, f_real, y_full, y_real, h_full, h_real):
    for i in range(2):
        h_real[i] = both(f_real[i], y_real[i])

    def step(k, carry):
        h_full[k] = both(f_full[k], y_full[k])
        return carry

    lax.fori_loop(0, HALF - 1, step, 0)


def filtered(inner, f_full, f_real, g_full, g_real, y_full, y_real, h_full, h_real):
    length = inner * RADIX

    def product(a, b, size):
        ar, ai, br, bi = a[:size], a[size:], b[:size], b[size:]
        return ar * br - ai * bi, ar * bi + ai * br

    for i in range(2):
        half = inner // 2
        a, b = both(f_real[i], y_real[i]), h_real[i]
        pr, pi = product(a, b, half)
        pr, pi = pr * (2.0 / length), pi * (2.0 / length)
        if i == 0:
            top = lax.broadcasted_iota(jnp.int32, pr.shape, 0) == 0
            pr = jnp.where(top, a[:half] * b[:half] * (1.0 / length), pr)
            pi = jnp.where(top, a[half:] * b[half:] * (1.0 / length), pi)
        z = jnp.concatenate([pr, pi]).astype(jnp.bfloat16)
        h_real[i] = both(g_real[i], z)

    def step(k, carry):
        pr, pi = product(both(f_full[k], y_full[k]), h_full[k], inner)
        z = (jnp.concatenate([pr, pi]) * (2.0 / length)).astype(jnp.bfloat16)
        h_full[k] = both(g_full[k], z)
        return carry

    lax.fori_loop(0, HALF - 1, step, 0)


def gather_blocks(inner, h_full, h_real, store):
    def step(i, carry):
        start = pl.multiple_of(i * CHUNK, CHUNK)
        rows = pl.ds(start, CHUNK)
        lower = pl.ds(pl.multiple_of(inner + start, CHUNK), CHUNK)
        u = {0: h_real[0, rows, :], HALF: h_real[1, rows, :]}
        for k in range(1, HALF):
            u[k] = (h_full[k - 1, rows, :], h_full[k - 1, lower, :])
        for n, block in enumerate(block_idft(u)):
            store(n, start, block.astype(jnp.bfloat16))
        return carry

    lax.fori_loop(0, inner // CHUNK, step, 0)


def spectrum_scratch(inner):
    wide = (HALF - 1, 2 * inner, LANES)
    return [
        pltpu.VMEM(wide, jnp.bfloat16),
        pltpu.VMEM((2, inner, LANES), jnp.bfloat16),
        pltpu.VMEM(wide, jnp.float32),
        pltpu.VMEM((2, inner, LANES), jnp.float32),
    ]


highest_precision = lax.Precision.HIGHEST


def shifted(block, axis, distance):
    devices = range(lax.axis_size(axis))
    route = [(i - distance, i) for i in devices if i - distance in devices]
    return lax.ppermute(block, axis, route)


def for_sending(value):
    return jax.tree.map(lambda a: a.astype(jnp.bfloat16) if a.dtype == jnp.float32 else a, value)


def angle_table(count, left, right):
    product = left[:, None] * right[None, :] % count
    angle = product.astype(jnp.float32) * (2.0 * math.pi / count)
    return (jnp.cos(angle), jnp.sin(angle))


def contract(pattern, table, values):
    return jnp.einsum(pattern, table, values, precision=highest_precision)


def rotate(pattern, cos_table, sin_table, real_part, imag_part, turning):
    out_real = contract(pattern, cos_table, real_part) - turning * contract(
        pattern, sin_table, imag_part
    )
    out_imag = contract(pattern, cos_table, imag_part) + turning * contract(
        pattern, sin_table, real_part
    )
    return (out_real, out_imag)


def frequency_order(groups):
    return jnp.arange(2 * groups, dtype=jnp.int32)


def shards(q_proj, k_proj, v_proj, feat_filter, long_filter, skip_bias, norm_gain):
    rows = q_proj.shape[0]
    taps = feat_filter.shape[1]
    groups = lax.axis_size("seq")
    stacked = jnp.stack([q_proj, k_proj, v_proj])
    previous = shifted(stacked[:, rows - (taps - 1) :, :], "seq", 1)
    extended = jnp.concatenate([previous, stacked], axis=1)
    featured = jnp.zeros(stacked.shape, jnp.float32)
    for offset in range(taps):
        window = extended[:, taps - 1 - offset : taps - 1 - offset + rows, :]
        featured = featured + feat_filter[:, offset, None, :] * window.astype(jnp.float32)
    query = featured[0]
    gated = featured[1] * featured[2]
    device = lax.axis_index("seq")
    per_device = rows // groups
    length = 2 * rows * groups
    order = frequency_order(groups)
    blocks = jnp.arange(groups, dtype=jnp.int32)
    within = jnp.arange(rows, dtype=jnp.int32)
    local_rows = device * per_device + jnp.arange(per_device, dtype=jnp.int32)
    slots = lax.dynamic_slice_in_dim(order, 2 * device, 2)
    cos_a, sin_a = angle_table(2 * groups, order, blocks)
    cos_w, sin_w = angle_table(length, order, local_rows)
    cos_b, sin_b = angle_table(rows, within, within)
    cos_v, sin_v = angle_table(length, slots, within)
    cos_i, sin_i = angle_table(2 * groups, blocks, order)
    signals = jnp.stack([gated, long_filter])[:, None]
    pieces = lax.all_to_all(
        signals.astype(jnp.bfloat16), "seq", split_axis=2, concat_axis=1, tiled=True
    ).astype(signals.dtype)
    real_part = contract("ka,xabc->xkbc", cos_a, pieces)
    imag_part = -contract("ka,xabc->xkbc", sin_a, pieces)
    cosine = cos_w[:, :, None]
    sine = sin_w[:, :, None]
    real_part, imag_part = (
        real_part * cosine + imag_part * sine,
        imag_part * cosine - real_part * sine,
    )
    spread = jnp.stack([real_part, imag_part], axis=1)
    pieces = lax.all_to_all(
        for_sending(spread), "seq", split_axis=2, concat_axis=3, tiled=True
    ).astype(spread.dtype)
    real_part, imag_part = rotate("kb,xsbc->xskc", cos_b, sin_b, pieces[:, 0], pieces[:, 1], -1.0)
    prod_real = real_part[0] * real_part[1] - imag_part[0] * imag_part[1]
    prod_imag = real_part[0] * imag_part[1] + imag_part[0] * real_part[1]
    real_part = prod_real
    imag_part = prod_imag
    real_part, imag_part = rotate("bk,skc->sbc", cos_b, sin_b, real_part, imag_part, 1.0)
    cosine = cos_v[:, :, None]
    sine = sin_v[:, :, None]
    spectra = jnp.stack(
        [real_part * cosine - imag_part * sine, imag_part * cosine + real_part * sine]
    )
    pieces = lax.all_to_all(
        for_sending(spectra), "seq", split_axis=2, concat_axis=1, tiled=True
    ).astype(spectra.dtype)
    summed = contract("ak,kbc->abc", cos_i, pieces[0]) - contract("ak,kbc->abc", sin_i, pieces[1])
    returned = summed / length
    long_conv = lax.all_to_all(
        for_sending(returned), "seq", split_axis=0, concat_axis=1, tiled=True
    ).astype(returned.dtype)[0]
    mixed = query * (long_conv + skip_bias * gated)
    squares = lax.psum(jnp.sum(mixed * mixed, axis=1), "ch")
    scale = lax.rsqrt(squares / D + 1e-05)
    normed = (mixed * scale[:, None] * norm_gain).astype(jnp.bfloat16)
    return (mixed.astype(jnp.bfloat16), normed)


def conv_kernel(inner, x_ref, f_full, f_real, g_full, g_real, o_ref, y_full, y_real, h_full, h_real):
    def load(which, n, start):
        rows = pl.ds(pl.multiple_of(n * inner + start, CHUNK), CHUNK)
        return x_ref[which, rows, :].astype(jnp.float32)

    def store(n, start, block):
        o_ref[pl.ds(pl.multiple_of(n * inner + start, CHUNK), CHUNK), :] = block

    spread_blocks(inner, functools.partial(load, 1), y_full, y_real)
    filter_spectrum(f_full, f_real, y_full, y_real, h_full, h_real)
    spread_blocks(inner, functools.partial(load, 0), y_full, y_real)
    filtered(inner, f_full, f_real, g_full, g_real, y_full, y_real, h_full, h_real)
    gather_blocks(inner, h_full, h_real, store)


def long_convolution(signals, seq):
    inner = seq // HALF
    tables = [jnp.asarray(t) for t in dft_tables(seq)]
    return pl.pallas_call(
        functools.partial(conv_kernel, inner),
        out_shape=jax.ShapeDtypeStruct((seq, LANES), jnp.bfloat16),
        in_specs=[pl.BlockSpec(memory_space=pltpu.VMEM)] * 5,
        out_specs=pl.BlockSpec(memory_space=pltpu.VMEM),
        scratch_shapes=spectrum_scratch(inner),
        compiler_params=pltpu.CompilerParams(vmem_limit_bytes=48 * 2**20),
    )(signals, *tables)


def channel_shards(q_proj, k_proj, v_proj, feat_filter, long_filter, skip_bias, norm_gain):
    rows = q_proj.shape[0]
    taps = feat_filter.shape[1]
    seq = rows * lax.axis_size("seq")
    stacked = jnp.stack([q_proj, k_proj, v_proj])
    previous = shifted(stacked[:, rows - (taps - 1) :, :], "seq", 1)
    extended = jnp.concatenate([previous, stacked], axis=1)
    featured = jnp.zeros(stacked.shape, jnp.float32)
    for offset in range(taps):
        window = extended[:, taps - 1 - offset : taps - 1 - offset + rows, :]
        featured = featured + feat_filter[:, offset, None, :] * window.astype(jnp.float32)
    query = featured[0]
    gated = featured[1] * featured[2]
    signals = jnp.stack([gated, long_filter]).astype(jnp.bfloat16)
    pieces = lax.all_to_all(signals, "seq", split_axis=2, concat_axis=1, tiled=True)
    returned = long_convolution(pieces, seq)
    long_conv = lax.all_to_all(returned, "seq", split_axis=0, concat_axis=1, tiled=True)
    mixed = query * (long_conv.astype(jnp.float32) + skip_bias * gated)
    squares = lax.psum(jnp.sum(mixed * mixed, axis=1), "ch")
    scale = lax.rsqrt(squares / D + 1e-05)
    normed = (mixed * scale[:, None] * norm_gain).astype(jnp.bfloat16)
    return (mixed.astype(jnp.bfloat16), normed)


def solution(mesh):
    def layer(*arrays):
        rows, channels = arrays[0].shape
        seq = rows * mesh.shape["seq"]
        whole_lanes = channels == LANES * mesh.shape["seq"]
        if whole_lanes and seq % (HALF * 256) == 0 and seq <= 2048:
            return channel_shards(*arrays)
        return shards(*arrays)

    return jax.shard_map(
        layer,
        mesh=mesh,
        in_specs=(
            P("seq", "ch"),
            P("seq", "ch"),
            P("seq", "ch"),
            P(None, None, "ch"),
            P("seq", "ch"),
            P("ch"),
            P("ch"),
        ),
        out_specs=(P("seq", "ch"), P("seq", "ch")),
        check_vma=False,
    )
```

```python
import functools
import math

import jax
import jax.numpy as jnp
import numpy as np
from jax import lax
from jax.experimental import pallas as pl
from jax.experimental.pallas import tpu as pltpu
from jax.sharding import PartitionSpec as P

D = 4096
RADIX = 16
HALF = RADIX // 2
LANES = 128
MESH = pl.DeviceIdType.MESH


def dft_tables(seq):
    length = 2 * seq
    inner = length // RADIX
    tokens = np.arange(inner, dtype=np.int64)

    def waves(freq):
        angle = (freq[:, None] * tokens[None, :] % length) * (2.0 * math.pi / length)
        return np.cos(angle), np.sin(angle)

    full = []
    for k1 in range(1, HALF):
        c, s = waves(k1 + RADIX * np.arange(inner, dtype=np.int64))
        full.append(np.block([[c, s], [-s, c]]))
    real = []
    for k1 in (0, HALF):
        c, s = waves(k1 + RADIX * np.arange(inner // 2, dtype=np.int64))
        table = np.concatenate([c, -s])
        if k1 == 0:
            table[inner // 2] = np.cos(math.pi * tokens)
        real.append(table)

    def split(table):
        high = table.astype(jnp.bfloat16)
        low = (table - high.astype(np.float64)).astype(jnp.bfloat16)
        return np.concatenate([high, low], axis=-1)

    full, real = np.stack(full), np.stack(real)
    turn = lambda a: np.swapaxes(a, 1, 2)
    return split(full), split(real), split(turn(full)), split(turn(real))


def turned(cr, ci, a):
    return (cr * a[0] - ci * a[1], cr * a[1] + ci * a[0])


def unit(power):
    angle = 2.0 * math.pi * power / RADIX
    return math.cos(angle), math.sin(angle)


def block_dft(x):
    s = math.sqrt(0.5)
    a = [x[n] + x[n + 4] for n in range(4)]
    b = [x[n] - x[n + 4] for n in range(4)]
    out = {}
    e, o = a[0] + a[2], a[1] + a[3]
    out[0], out[8] = e + o, e - o
    out[4] = (a[0] - a[2], a[3] - a[1])
    d, m = s * (b[1] - b[3]), s * (b[1] + b[3])
    out[2] = (b[0] + d, -b[2] - m)
    out[6] = (b[0] - d, b[2] - m)
    for first, sign in ((1, -1.0), (3, 1.0)):
        t = [(x[0], sign * x[4])]
        for n in range(1, 4):
            cr, ci = unit(-first * n)
            t.append(turned(cr, ci, (x[n], sign * x[n + 4])))
        er, ei = t[0][0] + t[2][0], t[0][1] + t[2][1]
        dr, di = t[0][0] - t[2][0], t[0][1] - t[2][1]
        fr, fi = t[1][0] + t[3][0], t[1][1] + t[3][1]
        gr, gi = t[1][0] - t[3][0], t[1][1] - t[3][1]
        out[first] = (er + fr, ei + fi)
        out[first + 4] = (dr + gi, di - gr)
    return out


def block_idft(u):
    s = math.sqrt(0.5)
    p, m = u[0] + u[8], u[0] - u[8]
    a = [p + u[4][0], m - u[4][1], p - u[4][0], m + u[4][1]]
    b = [
        u[2][0] + u[6][0],
        s * ((u[2][0] - u[2][1]) - (u[6][0] + u[6][1])),
        u[6][1] - u[2][1],
        s * ((u[6][0] - u[6][1]) - (u[2][0] + u[2][1])),
    ]
    out = [None] * HALF
    for n in range(4):
        low, high = a[n] + b[n], a[n] - b[n]
        for first, sign in ((1, -1.0), (3, 1.0)):
            v, w = u[first], u[first + 4]
            if n == 0:
                v = (v[0] + w[0], v[1] + w[1])
            elif n == 1:
                v = (v[0] - w[1], v[1] + w[0])
            elif n == 2:
                v = (v[0] - w[0], v[1] - w[1])
            else:
                v = (v[0] + w[1], v[1] - w[0])
            q = turned(*unit(first * n), v)
            low, high = low + q[0], high + sign * q[1]
        out[n], out[n + 4] = low, high
    return out


CHUNK = 32


def spread_blocks(inner, load, y_full, y_real):
    def step(i, carry):
        start = pl.multiple_of(i * CHUNK, CHUNK)
        rows = pl.ds(start, CHUNK)
        out = block_dft([load(n, start) for n in range(HALF)])
        y_real[0, rows, :] = out[0].astype(jnp.bfloat16)
        y_real[1, rows, :] = out[HALF].astype(jnp.bfloat16)
        lower = pl.ds(pl.multiple_of(inner + start, CHUNK), CHUNK)
        for k in range(1, HALF):
            y_full[k - 1, rows, :] = out[k][0].astype(jnp.bfloat16)
            y_full[k - 1, lower, :] = out[k][1].astype(jnp.bfloat16)
        return carry

    lax.fori_loop(0, inner // CHUNK, step, 0)


def both(table, values):
    half = table.shape[1] // 2
    first = jnp.dot(table[:, :half], values, preferred_element_type=jnp.float32)
    return first + jnp.dot(table[:, half:], values, preferred_element_type=jnp.float32)


def filter_spectrum(f_full, f_real, y_full, y_real, h_full, h_real):
    for i in range(2):
        h_real[i] = both(f_real[i], y_real[i])

    def step(k, carry):
        h_full[k] = both(f_full[k], y_full[k])
        return carry

    lax.fori_loop(0, HALF - 1, step, 0)


def filtered(inner, f_full, f_real, g_full, g_real, y_full, y_real, h_full, h_real):
    length = inner * RADIX

    def product(a, b, size):
        ar, ai, br, bi = a[:size], a[size:], b[:size], b[size:]
        return ar * br - ai * bi, ar * bi + ai * br

    for i in range(2):
        half = inner // 2
        a, b = both(f_real[i], y_real[i]), h_real[i]
        pr, pi = product(a, b, half)
        pr, pi = pr * (2.0 / length), pi * (2.0 / length)
        if i == 0:
            top = lax.broadcasted_iota(jnp.int32, pr.shape, 0) == 0
            pr = jnp.where(top, a[:half] * b[:half] * (1.0 / length), pr)
            pi = jnp.where(top, a[half:] * b[half:] * (1.0 / length), pi)
        z = jnp.concatenate([pr, pi]).astype(jnp.bfloat16)
        h_real[i] = both(g_real[i], z)

    def step(k, carry):
        pr, pi = product(both(f_full[k], y_full[k]), h_full[k], inner)
        z = (jnp.concatenate([pr, pi]) * (2.0 / length)).astype(jnp.bfloat16)
        h_full[k] = both(g_full[k], z)
        return carry

    lax.fori_loop(0, HALF - 1, step, 0)


def gather_blocks(inner, h_full, h_real, store):
    def step(i, carry):
        start = pl.multiple_of(i * CHUNK, CHUNK)
        rows = pl.ds(start, CHUNK)
        lower = pl.ds(pl.multiple_of(inner + start, CHUNK), CHUNK)
        u = {0: h_real[0, rows, :], HALF: h_real[1, rows, :]}
        for k in range(1, HALF):
            u[k] = (h_full[k - 1, rows, :], h_full[k - 1, lower, :])
        for n, block in enumerate(block_idft(u)):
            store(n, start, block.astype(jnp.bfloat16))
        return carry

    lax.fori_loop(0, inner // CHUNK, step, 0)


def spectrum_scratch(inner):
    wide = (HALF - 1, 2 * inner, LANES)
    return [
        pltpu.VMEM(wide, jnp.bfloat16),
        pltpu.VMEM((2, inner, LANES), jnp.bfloat16),
        pltpu.VMEM(wide, jnp.float32),
        pltpu.VMEM((2, inner, LANES), jnp.float32),
    ]


highest_precision = lax.Precision.HIGHEST


def shifted(block, axis, distance):
    devices = range(lax.axis_size(axis))
    route = [(i - distance, i) for i in devices if i - distance in devices]
    return lax.ppermute(block, axis, route)


def for_sending(value):
    return jax.tree.map(lambda a: a.astype(jnp.bfloat16) if a.dtype == jnp.float32 else a, value)


def angle_table(count, left, right):
    product = left[:, None] * right[None, :] % count
    angle = product.astype(jnp.float32) * (2.0 * math.pi / count)
    return (jnp.cos(angle), jnp.sin(angle))


def contract(pattern, table, values):
    return jnp.einsum(pattern, table, values, precision=highest_precision)


def rotate(pattern, cos_table, sin_table, real_part, imag_part, turning):
    out_real = contract(pattern, cos_table, real_part) - turning * contract(
        pattern, sin_table, imag_part
    )
    out_imag = contract(pattern, cos_table, imag_part) + turning * contract(
        pattern, sin_table, real_part
    )
    return (out_real, out_imag)


def frequency_order(groups):
    return jnp.arange(2 * groups, dtype=jnp.int32)


def shards(q_proj, k_proj, v_proj, feat_filter, long_filter, skip_bias, norm_gain):
    rows = q_proj.shape[0]
    taps = feat_filter.shape[1]
    groups = lax.axis_size("seq")
    stacked = jnp.stack([q_proj, k_proj, v_proj])
    previous = shifted(stacked[:, rows - (taps - 1) :, :], "seq", 1)
    extended = jnp.concatenate([previous, stacked], axis=1)
    featured = jnp.zeros(stacked.shape, jnp.float32)
    for offset in range(taps):
        window = extended[:, taps - 1 - offset : taps - 1 - offset + rows, :]
        featured = featured + feat_filter[:, offset, None, :] * window.astype(jnp.float32)
    query = featured[0]
    gated = featured[1] * featured[2]
    device = lax.axis_index("seq")
    per_device = rows // groups
    length = 2 * rows * groups
    order = frequency_order(groups)
    blocks = jnp.arange(groups, dtype=jnp.int32)
    within = jnp.arange(rows, dtype=jnp.int32)
    local_rows = device * per_device + jnp.arange(per_device, dtype=jnp.int32)
    slots = lax.dynamic_slice_in_dim(order, 2 * device, 2)
    cos_a, sin_a = angle_table(2 * groups, order, blocks)
    cos_w, sin_w = angle_table(length, order, local_rows)
    cos_b, sin_b = angle_table(rows, within, within)
    cos_v, sin_v = angle_table(length, slots, within)
    cos_i, sin_i = angle_table(2 * groups, blocks, order)
    signals = jnp.stack([gated, long_filter])[:, None]
    pieces = lax.all_to_all(
        signals.astype(jnp.bfloat16), "seq", split_axis=2, concat_axis=1, tiled=True
    ).astype(signals.dtype)
    real_part = contract("ka,xabc->xkbc", cos_a, pieces)
    imag_part = -contract("ka,xabc->xkbc", sin_a, pieces)
    cosine = cos_w[:, :, None]
    sine = sin_w[:, :, None]
    real_part, imag_part = (
        real_part * cosine + imag_part * sine,
        imag_part * cosine - real_part * sine,
    )
    spread = jnp.stack([real_part, imag_part], axis=1)
    pieces = lax.all_to_all(
        for_sending(spread), "seq", split_axis=2, concat_axis=3, tiled=True
    ).astype(spread.dtype)
    real_part, imag_part = rotate("kb,xsbc->xskc", cos_b, sin_b, pieces[:, 0], pieces[:, 1], -1.0)
    prod_real = real_part[0] * real_part[1] - imag_part[0] * imag_part[1]
    prod_imag = real_part[0] * imag_part[1] + imag_part[0] * real_part[1]
    real_part = prod_real
    imag_part = prod_imag
    real_part, imag_part = rotate("bk,skc->sbc", cos_b, sin_b, real_part, imag_part, 1.0)
    cosine = cos_v[:, :, None]
    sine = sin_v[:, :, None]
    spectra = jnp.stack(
        [real_part * cosine - imag_part * sine, imag_part * cosine + real_part * sine]
    )
    pieces = lax.all_to_all(
        for_sending(spectra), "seq", split_axis=2, concat_axis=1, tiled=True
    ).astype(spectra.dtype)
    summed = contract("ak,kbc->abc", cos_i, pieces[0]) - contract("ak,kbc->abc", sin_i, pieces[1])
    returned = summed / length
    long_conv = lax.all_to_all(
        for_sending(returned), "seq", split_axis=0, concat_axis=1, tiled=True
    ).astype(returned.dtype)[0]
    mixed = query * (long_conv + skip_bias * gated)
    squares = lax.psum(jnp.sum(mixed * mixed, axis=1), "ch")
    scale = lax.rsqrt(squares / D + 1e-05)
    normed = (mixed * scale[:, None] * norm_gain).astype(jnp.bfloat16)
    return (mixed.astype(jnp.bfloat16), normed)


def mixer_kernel(
    n, inner,
    q_hbm, k_hbm, v_hbm, filter_hbm, f_full_hbm, f_real_hbm, g_full_hbm, g_real_hbm,
    feat_ref, skip_ref, gain_ref,
    mixed_ref, normed_ref,
    q_ref, k_ref, v_ref, filter_ref, f_full, f_real, g_full, g_real,
    tails, send_f, send_g, send_y, recv_f, recv_g, recv_y, query, gated, sums, other_sums,
    y_full, y_real, h_full, h_real,
    local_sem, tail_send, tail_recv, f_send, f_recv, g_send, g_recv, y_send, y_recv, sum_sem,
):
    me = lax.axis_index("seq")
    core = lax.axis_index("ch")
    other = 1 - core
    rows = q_ref.shape[0]
    after = lax.rem(me + 1, n)

    def at(block):
        return pl.ds(pl.multiple_of(block * rows, rows), rows)

    def lanes(block):
        return pl.ds(pl.multiple_of(block * LANES, LANES), LANES)

    def partner(j):
        offset = n // 2 + ((j + 1) // 2) * (2 * (j % 2) - 1)
        return lax.rem(me + offset, n)

    loads = [
        pltpu.make_async_copy(source, target, local_sem.at[i])
        for i, (source, target) in enumerate([
            (filter_hbm, filter_ref), (k_hbm, k_ref), (v_hbm, v_ref), (q_hbm, q_ref),
            (f_real_hbm, f_real), (f_full_hbm, f_full), (g_real_hbm, g_real), (g_full_hbm, g_full),
        ])
    ]
    for load in loads:
        load.start()

    barrier = pltpu.get_barrier_semaphore()

    def greet(j, carry):
        pl.semaphore_signal(
            barrier, inc=1, device_id=(partner(j), core), device_id_type=MESH
        )
        return carry

    lax.fori_loop(0, n - 1, greet, 0)
    pl.semaphore_signal(barrier, inc=1, device_id=(me, other), device_id_type=MESH)

    loads[0].wait()

    def narrow(j, carry):
        send_f[at(j), :] = filter_ref[:, lanes(j)].astype(jnp.bfloat16)
        return carry

    lax.fori_loop(0, n, narrow, 0)
    recv_f[at(me), :] = send_f[at(me), :]
    for load in loads[1:4]:
        load.wait()
    pl.semaphore_wait(barrier, n)

    def tail_copy(i, ref):
        return pltpu.make_async_remote_copy(
            src_ref=ref.at[pl.ds(rows - 16, 16), :],
            dst_ref=tails.at[i],
            send_sem=tail_send.at[i],
            recv_sem=tail_recv.at[i],
            device_id=(after, core),
            device_id_type=MESH,
        )

    tail_copies = [tail_copy(i, ref) for i, ref in enumerate((k_ref, v_ref, q_ref))]
    for copy in tail_copies:
        copy.start()

    def exchange(source, target, send_sem, recv_sem):
        def to(peer):
            return pltpu.make_async_remote_copy(
                src_ref=source.at[at(peer), :],
                dst_ref=target.at[at(me), :],
                send_sem=send_sem.at[peer],
                recv_sem=recv_sem.at[me],
                device_id=(peer, core),
                device_id_type=MESH,
            )

        def come(peer):
            return pltpu.make_async_remote_copy(
                src_ref=source.at[at(peer), :],
                dst_ref=target.at[at(peer), :],
                send_sem=send_sem.at[peer],
                recv_sem=recv_sem.at[peer],
                device_id=(peer, core),
                device_id_type=MESH,
            )

        def start(j, carry):
            to(partner(j)).start()
            return carry

        def arrive(j, carry):
            come(partner(n - 2 - j)).wait_recv()
            return carry

        def leave(j, carry):
            to(partner(j)).wait_send()
            return carry

        return (
            lambda: lax.fori_loop(0, n - 1, start, 0),
            lambda: lax.fori_loop(0, n - 1, arrive, 0),
            lambda: lax.fori_loop(0, n - 1, leave, 0),
        )

    start_f, arrive_f, leave_f = exchange(send_f, recv_f, f_send, f_recv)
    start_g, arrive_g, leave_g = exchange(send_g, recv_g, g_send, g_recv)
    start_y, arrive_y, leave_y = exchange(send_y, recv_y, y_send, y_recv)
    start_f()

    first = me == 0

    def featured(stream, tail, ref, j):
        columns = lanes(j)
        before = tails[tail, :, columns].astype(jnp.float32)
        before = jnp.where(first, 0.0, before)
        window = jnp.concatenate([before, ref[:, columns].astype(jnp.float32)])
        total = feat_ref[3 * stream, :, columns] * window[16:]
        for tap in (1, 2):
            moved = pltpu.roll(window, tap, 0)[16:]
            total = total + feat_ref[3 * stream + tap, :, columns] * moved
        return total

    for copy in tail_copies[:2]:
        copy.wait()

    def gate(j, carry):
        value = featured(1, 0, k_ref, j) * featured(2, 1, v_ref, j)
        gated[at(j), :] = value
        send_g[at(j), :] = value.astype(jnp.bfloat16)
        return carry

    lax.fori_loop(0, n, gate, 0)
    start_g()
    recv_g[at(me), :] = send_g[at(me), :]
    tail_copies[2].wait()

    def ask(j, carry):
        query[at(j), :] = featured(0, 2, q_ref, j)
        return carry

    lax.fori_loop(0, n, ask, 0)

    def block_of(ref):
        def load(block, start):
            where = pl.ds(pl.multiple_of(block * inner + start, CHUNK), CHUNK)
            return ref[where, :].astype(jnp.float32)

        return load

    def store(block, start, value):
        send_y[pl.ds(pl.multiple_of(block * inner + start, CHUNK), CHUNK), :] = value

    for load in loads[4:]:
        load.wait()
    arrive_f()
    spread_blocks(inner, block_of(recv_f), y_full, y_real)
    filter_spectrum(f_full, f_real, y_full, y_real, h_full, h_real)
    arrive_g()
    spread_blocks(inner, block_of(recv_g), y_full, y_real)
    filtered(inner, f_full, f_real, g_full, g_real, y_full, y_real, h_full, h_real)
    gather_blocks(inner, h_full, h_real, store)
    start_y()
    recv_y[at(me), :] = send_y[at(me), :]
    leave_f()
    leave_g()
    arrive_y()

    def mix(j, carry):
        conv = recv_y[at(j), :].astype(jnp.float32)
        mixed = query[at(j), :] * (conv + skip_ref[:, lanes(j)] * gated[at(j), :])
        query[at(j), :] = mixed
        mixed_ref[:, lanes(j)] = mixed.astype(jnp.bfloat16)
        return carry + mixed * mixed

    squares = lax.fori_loop(0, n, mix, jnp.zeros((rows, LANES), jnp.float32))
    sums[...] = squares
    sum_copy = pltpu.make_async_remote_copy(
        src_ref=sums,
        dst_ref=other_sums,
        send_sem=sum_sem.at[0],
        recv_sem=sum_sem.at[1],
        device_id=(me, other),
        device_id_type=MESH,
    )
    sum_copy.start()
    leave_y()
    sum_copy.wait()
    total = jnp.sum(sums[...] + other_sums[...], axis=1, keepdims=True)
    scale = lax.rsqrt(total / D + 1e-05)

    def norm(j, carry):
        value = query[at(j), :] * scale * gain_ref[:, lanes(j)]
        normed_ref[:, lanes(j)] = value.astype(jnp.bfloat16)
        return carry

    lax.fori_loop(0, n, norm, 0)


def channel_shards(q_proj, k_proj, v_proj, feat_filter, long_filter, skip_bias, norm_gain):
    rows, channels = q_proj.shape
    n = lax.axis_size("seq")
    seq = rows * n
    inner = seq // HALF
    tables = [jnp.asarray(t) for t in dft_tables(seq)]
    narrow, wide = jnp.bfloat16, jnp.float32
    scratch = [pltpu.VMEM((rows, channels), narrow)] * 3 + [pltpu.VMEM((rows, channels), wide)]
    scratch += [pltpu.VMEM(t.shape, narrow) for t in tables]
    scratch += [pltpu.VMEM((3, 16, channels), narrow)]
    scratch += [pltpu.VMEM((seq, LANES), narrow)] * 6
    scratch += [pltpu.VMEM((seq, LANES), wide)] * 2
    scratch += [pltpu.VMEM((rows, LANES), wide)] * 2
    scratch += spectrum_scratch(inner)
    scratch += [pltpu.SemaphoreType.DMA((8,))]
    scratch += [pltpu.SemaphoreType.DMA((3,))] * 2
    scratch += [pltpu.SemaphoreType.DMA((n,))] * 6
    scratch += [pltpu.SemaphoreType.DMA((2,))]
    whole = pl.BlockSpec(memory_space=pltpu.VMEM)
    away = pl.BlockSpec(memory_space=pl.ANY)
    out = jax.ShapeDtypeStruct((rows, channels), narrow)
    return tuple(pl.pallas_call(
        functools.partial(mixer_kernel, n, inner),
        out_shape=(out, out),
        in_specs=[away] * 8 + [whole] * 3,
        out_specs=(whole, whole),
        scratch_shapes=scratch,
        compiler_params=pltpu.CompilerParams(
            collective_id=0, has_side_effects=True, vmem_limit_bytes=48 * 2**20
        ),
    )(
        q_proj, k_proj, v_proj, long_filter, *tables,
        feat_filter.reshape(-1, 1, channels), skip_bias.reshape(1, -1), norm_gain.reshape(1, -1),
    ))


def solution(mesh):
    def layer(*arrays):
        rows, channels = arrays[0].shape
        n = mesh.shape["seq"]
        seq = rows * n
        whole_lanes = channels == LANES * n and n % 2 == 0 and mesh.shape["ch"] == 2
        if whole_lanes and rows % 16 == 0 and seq % (2 * HALF * CHUNK) == 0 and seq <= 2048:
            return channel_shards(*arrays)
        return shards(*arrays)

    return jax.shard_map(
        layer,
        mesh=mesh,
        in_specs=(
            P("seq", "ch"),
            P("seq", "ch"),
            P("seq", "ch"),
            P(None, None, "ch"),
            P("seq", "ch"),
            P("ch"),
            P("ch"),
        ),
        out_specs=(P("seq", "ch"), P("seq", "ch")),
        check_vma=False,
    )
```

```python
import functools
import math

import jax
import jax.numpy as jnp
import numpy as np
from jax import lax
from jax.experimental import pallas as pl
from jax.experimental.pallas import tpu as pltpu
from jax.sharding import PartitionSpec as P

D = 4096
RADIX = 16
HALF = RADIX // 2
LANES = 128
VMEM_BYTES = 62 * 2**20
MESH = pl.DeviceIdType.MESH


def dft_tables(seq):
    length = 2 * seq
    inner = length // RADIX
    tokens = np.arange(inner, dtype=np.int64)

    def waves(freq):
        angle = (freq[:, None] * tokens[None, :] % length) * (2.0 * math.pi / length)
        return np.cos(angle), np.sin(angle)

    full = []
    for k1 in range(1, HALF):
        c, s = waves(k1 + RADIX * np.arange(inner, dtype=np.int64))
        full.append(np.block([[c, s], [-s, c]]))
    real = []
    for k1 in (0, HALF):
        c, s = waves(k1 + RADIX * np.arange(inner // 2, dtype=np.int64))
        table = np.concatenate([c, -s])
        if k1 == 0:
            table[inner // 2] = np.cos(math.pi * tokens)
        real.append(table)

    def split(table):
        high = table.astype(jnp.bfloat16)
        low = (table - high.astype(np.float64)).astype(jnp.bfloat16)
        return np.concatenate([high, low], axis=-1)

    full, real = np.stack(full), np.stack(real)
    turn = lambda a: np.swapaxes(a, 1, 2)
    return split(full), split(real), turn(full).astype(jnp.bfloat16), turn(real).astype(jnp.bfloat16)


def turned(cr, ci, a):
    return (cr * a[0] - ci * a[1], cr * a[1] + ci * a[0])


def unit(power):
    angle = 2.0 * math.pi * power / RADIX
    return math.cos(angle), math.sin(angle)


def block_dft(x):
    s = math.sqrt(0.5)
    a = [x[n] + x[n + 4] for n in range(4)]
    b = [x[n] - x[n + 4] for n in range(4)]
    out = {}
    e, o = a[0] + a[2], a[1] + a[3]
    out[0], out[8] = e + o, e - o
    out[4] = (a[0] - a[2], a[3] - a[1])
    d, m = s * (b[1] - b[3]), s * (b[1] + b[3])
    out[2] = (b[0] + d, -b[2] - m)
    out[6] = (b[0] - d, b[2] - m)
    for first, sign in ((1, -1.0), (3, 1.0)):
        t = [(x[0], sign * x[4])]
        for n in range(1, 4):
            cr, ci = unit(-first * n)
            t.append(turned(cr, ci, (x[n], sign * x[n + 4])))
        er, ei = t[0][0] + t[2][0], t[0][1] + t[2][1]
        dr, di = t[0][0] - t[2][0], t[0][1] - t[2][1]
        fr, fi = t[1][0] + t[3][0], t[1][1] + t[3][1]
        gr, gi = t[1][0] - t[3][0], t[1][1] - t[3][1]
        out[first] = (er + fr, ei + fi)
        out[first + 4] = (dr + gi, di - gr)
    return out


def block_idft(u):
    s = math.sqrt(0.5)
    p, m = u[0] + u[8], u[0] - u[8]
    a = [p + u[4][0], m - u[4][1], p - u[4][0], m + u[4][1]]
    b = [
        u[2][0] + u[6][0],
        s * ((u[2][0] - u[2][1]) - (u[6][0] + u[6][1])),
        u[6][1] - u[2][1],
        s * ((u[6][0] - u[6][1]) - (u[2][0] + u[2][1])),
    ]
    out = [None] * HALF
    for n in range(4):
        low, high = a[n] + b[n], a[n] - b[n]
        for first, sign in ((1, -1.0), (3, 1.0)):
            v, w = u[first], u[first + 4]
            if n == 0:
                v = (v[0] + w[0], v[1] + w[1])
            elif n == 1:
                v = (v[0] - w[1], v[1] + w[0])
            elif n == 2:
                v = (v[0] - w[0], v[1] - w[1])
            else:
                v = (v[0] + w[1], v[1] - w[0])
            q = turned(*unit(first * n), v)
            low, high = low + q[0], high + sign * q[1]
        out[n], out[n + 4] = low, high
    return out


CHUNK = 16


def spread_blocks(inner, load, y_full, y_real, rest=None):
    def put(ref, low_ref, k, rows, value):
        high = value.astype(jnp.bfloat16)
        ref[k, rows, :] = high
        if low_ref is not None:
            low_ref[k, rows, :] = (value - high.astype(jnp.float32)).astype(jnp.bfloat16)

    low_full, low_real = rest or (None, None)

    def step(i, carry):
        start = pl.multiple_of(i * CHUNK, CHUNK)
        rows = pl.ds(start, CHUNK)
        out = block_dft([load(n, start) for n in range(HALF)])
        put(y_real, low_real, 0, rows, out[0])
        put(y_real, low_real, 1, rows, out[HALF])
        lower = pl.ds(pl.multiple_of(inner + start, CHUNK), CHUNK)
        for k in range(1, HALF):
            put(y_full, low_full, k - 1, rows, out[k][0])
            put(y_full, low_full, k - 1, lower, out[k][1])
        return carry

    lax.fori_loop(0, inner // CHUNK, step, 0)


def dot(table, values):
    return jnp.dot(table, values, preferred_element_type=jnp.float32)


def careful(table, values, low):
    half = table.shape[1] // 2
    first = dot(table[:, :half], values) + dot(table[:, half:], values)
    return first + dot(table[:, :half], low)


def filter_spectrum(f_full, f_real, y_full, y_real, low_full, low_real, h_full, h_real):
    for i in range(2):
        h_real[i] = careful(f_real[i], y_real[i], low_real[i])

    def step(k, carry):
        h_full[k] = careful(f_full[k], y_full[k], low_full[k])
        return carry

    lax.fori_loop(0, HALF - 1, step, 0)


def filtered(inner, f_full, f_real, g_full, g_real, y_full, y_real, h_full, h_real):
    length = inner * RADIX

    def product(a, b, size):
        ar, ai, br, bi = a[:size], a[size:], b[:size], b[size:]
        return ar * br - ai * bi, ar * bi + ai * br

    for i in range(2):
        half = inner // 2
        a, b = dot(f_real[i, :, :inner], y_real[i]), h_real[i]
        pr, pi = product(a, b, half)
        pr, pi = pr * (2.0 / length), pi * (2.0 / length)
        if i == 0:
            top = lax.broadcasted_iota(jnp.int32, pr.shape, 0) == 0
            pr = jnp.where(top, a[:half] * b[:half] * (1.0 / length), pr)
            pi = jnp.where(top, a[half:] * b[half:] * (1.0 / length), pi)
        z = jnp.concatenate([pr, pi]).astype(jnp.bfloat16)
        h_real[i] = dot(g_real[i], z)

    def step(k, carry):
        pr, pi = product(dot(f_full[k, :, : 2 * inner], y_full[k]), h_full[k], inner)
        z = (jnp.concatenate([pr, pi]) * (2.0 / length)).astype(jnp.bfloat16)
        h_full[k] = dot(g_full[k], z)
        return carry

    lax.fori_loop(0, HALF - 1, step, 0)


def gather_blocks(inner, h_full, h_real, store):
    def step(i, carry):
        start = pl.multiple_of(i * CHUNK, CHUNK)
        rows = pl.ds(start, CHUNK)
        lower = pl.ds(pl.multiple_of(inner + start, CHUNK), CHUNK)
        u = {0: h_real[0, rows, :], HALF: h_real[1, rows, :]}
        for k in range(1, HALF):
            u[k] = (h_full[k - 1, rows, :], h_full[k - 1, lower, :])
        for n, block in enumerate(block_idft(u)):
            store(n, start, block.astype(jnp.bfloat16))
        return carry

    lax.fori_loop(0, inner // CHUNK, step, 0)


def spectrum_scratch(inner):
    wide = (HALF - 1, 2 * inner, LANES)
    return [
        pltpu.VMEM(wide, jnp.bfloat16),
        pltpu.VMEM((2, inner, LANES), jnp.bfloat16),
        pltpu.VMEM(wide, jnp.bfloat16),
        pltpu.VMEM((2, inner, LANES), jnp.bfloat16),
        pltpu.VMEM(wide, jnp.float32),
        pltpu.VMEM((2, inner, LANES), jnp.float32),
    ]


highest_precision = lax.Precision.HIGHEST


def shifted(block, axis, distance):
    devices = range(lax.axis_size(axis))
    route = [(i - distance, i) for i in devices if i - distance in devices]
    return lax.ppermute(block, axis, route)


def for_sending(value):
    return jax.tree.map(lambda a: a.astype(jnp.bfloat16) if a.dtype == jnp.float32 else a, value)


def angle_table(count, left, right):
    product = left[:, None] * right[None, :] % count
    angle = product.astype(jnp.float32) * (2.0 * math.pi / count)
    return (jnp.cos(angle), jnp.sin(angle))


def contract(pattern, table, values):
    return jnp.einsum(pattern, table, values, precision=highest_precision)


def rotate(pattern, cos_table, sin_table, real_part, imag_part, turning):
    out_real = contract(pattern, cos_table, real_part) - turning * contract(
        pattern, sin_table, imag_part
    )
    out_imag = contract(pattern, cos_table, imag_part) + turning * contract(
        pattern, sin_table, real_part
    )
    return (out_real, out_imag)


def frequency_order(groups):
    return jnp.arange(2 * groups, dtype=jnp.int32)


def shards(q_proj, k_proj, v_proj, feat_filter, long_filter, skip_bias, norm_gain):
    rows = q_proj.shape[0]
    taps = feat_filter.shape[1]
    groups = lax.axis_size("seq")
    stacked = jnp.stack([q_proj, k_proj, v_proj])
    previous = shifted(stacked[:, rows - (taps - 1) :, :], "seq", 1)
    extended = jnp.concatenate([previous, stacked], axis=1)
    featured = jnp.zeros(stacked.shape, jnp.float32)
    for offset in range(taps):
        window = extended[:, taps - 1 - offset : taps - 1 - offset + rows, :]
        featured = featured + feat_filter[:, offset, None, :] * window.astype(jnp.float32)
    query = featured[0]
    gated = featured[1] * featured[2]
    device = lax.axis_index("seq")
    per_device = rows // groups
    length = 2 * rows * groups
    order = frequency_order(groups)
    blocks = jnp.arange(groups, dtype=jnp.int32)
    within = jnp.arange(rows, dtype=jnp.int32)
    local_rows = device * per_device + jnp.arange(per_device, dtype=jnp.int32)
    slots = lax.dynamic_slice_in_dim(order, 2 * device, 2)
    cos_a, sin_a = angle_table(2 * groups, order, blocks)
    cos_w, sin_w = angle_table(length, order, local_rows)
    cos_b, sin_b = angle_table(rows, within, within)
    cos_v, sin_v = angle_table(length, slots, within)
    cos_i, sin_i = angle_table(2 * groups, blocks, order)
    signals = jnp.stack([gated, long_filter])[:, None]
    pieces = lax.all_to_all(
        signals.astype(jnp.bfloat16), "seq", split_axis=2, concat_axis=1, tiled=True
    ).astype(signals.dtype)
    real_part = contract("ka,xabc->xkbc", cos_a, pieces)
    imag_part = -contract("ka,xabc->xkbc", sin_a, pieces)
    cosine = cos_w[:, :, None]
    sine = sin_w[:, :, None]
    real_part, imag_part = (
        real_part * cosine + imag_part * sine,
        imag_part * cosine - real_part * sine,
    )
    spread = jnp.stack([real_part, imag_part], axis=1)
    pieces = lax.all_to_all(
        for_sending(spread), "seq", split_axis=2, concat_axis=3, tiled=True
    ).astype(spread.dtype)
    real_part, imag_part = rotate("kb,xsbc->xskc", cos_b, sin_b, pieces[:, 0], pieces[:, 1], -1.0)
    prod_real = real_part[0] * real_part[1] - imag_part[0] * imag_part[1]
    prod_imag = real_part[0] * imag_part[1] + imag_part[0] * real_part[1]
    real_part = prod_real
    imag_part = prod_imag
    real_part, imag_part = rotate("bk,skc->sbc", cos_b, sin_b, real_part, imag_part, 1.0)
    cosine = cos_v[:, :, None]
    sine = sin_v[:, :, None]
    spectra = jnp.stack(
        [real_part * cosine - imag_part * sine, imag_part * cosine + real_part * sine]
    )
    pieces = lax.all_to_all(
        for_sending(spectra), "seq", split_axis=2, concat_axis=1, tiled=True
    ).astype(spectra.dtype)
    summed = contract("ak,kbc->abc", cos_i, pieces[0]) - contract("ak,kbc->abc", sin_i, pieces[1])
    returned = summed / length
    long_conv = lax.all_to_all(
        for_sending(returned), "seq", split_axis=0, concat_axis=1, tiled=True
    ).astype(returned.dtype)[0]
    mixed = query * (long_conv + skip_bias * gated)
    squares = lax.psum(jnp.sum(mixed * mixed, axis=1), "ch")
    scale = lax.rsqrt(squares / D + 1e-05)
    normed = (mixed * scale[:, None] * norm_gain).astype(jnp.bfloat16)
    return (mixed.astype(jnp.bfloat16), normed)


def mixer_kernel(
    n, inner,
    q_hbm, k_hbm, v_hbm, filter_hbm, f_full_hbm, f_real_hbm, g_full_hbm, g_real_hbm,
    feat_hbm, skip_hbm,
    mixed_hbm, scale_ref,
    feat_ref, skip_ref, q_ref, k_ref, v_ref, filter_ref, f_full, f_real, g_full, g_real,
    tails, send_f, send_g, send_y, recv_f, recv_g, recv_y, query, gated, sums, other_sums,
    y_full, y_real, low_full, low_real, h_full, h_real,
    local_sem, tail_send, tail_recv, f_send, f_recv, g_send, g_recv, y_send, y_recv, sum_sem, out_sem,
):
    me = lax.axis_index("seq")
    core = lax.axis_index("ch")
    other = 1 - core
    rows = q_ref.shape[0]
    after = lax.rem(me + 1, n)

    def at(block):
        return pl.ds(pl.multiple_of(block * rows, rows), rows)

    def lanes(block):
        return pl.ds(pl.multiple_of(block * LANES, LANES), LANES)

    def partner(j):
        offset = n // 2 + ((j + 1) // 2) * (2 * (j % 2) - 1)
        return lax.rem(me + offset, n)

    loads = [
        pltpu.make_async_copy(source, target, local_sem.at[i])
        for i, (source, target) in enumerate([
            (filter_hbm, filter_ref), (k_hbm, k_ref), (v_hbm, v_ref), (q_hbm, q_ref),
            (feat_hbm, feat_ref), (skip_hbm, skip_ref),
            (f_real_hbm, f_real), (f_full_hbm, f_full), (g_real_hbm, g_real), (g_full_hbm, g_full),
        ])
    ]
    for load in loads[:6]:
        load.start()

    barrier = pltpu.get_barrier_semaphore()

    def greet(j, carry):
        pl.semaphore_signal(
            barrier, inc=1, device_id=(partner(j), core), device_id_type=MESH
        )
        return carry

    lax.fori_loop(0, n - 1, greet, 0)
    pl.semaphore_signal(barrier, inc=1, device_id=(me, other), device_id_type=MESH)

    loads[0].wait()

    def narrow(j, carry):
        send_f[at(j), :] = filter_ref[:, lanes(j)].astype(jnp.bfloat16)
        return carry

    lax.fori_loop(0, n, narrow, 0)
    recv_f[at(me), :] = send_f[at(me), :]
    for load in loads[1:6]:
        load.wait()
    pl.semaphore_wait(barrier, n)

    def tail_copy(i, ref):
        return pltpu.make_async_remote_copy(
            src_ref=ref.at[pl.ds(rows - 16, 16), :],
            dst_ref=tails.at[i],
            send_sem=tail_send.at[i],
            recv_sem=tail_recv.at[i],
            device_id=(after, core),
            device_id_type=MESH,
        )

    tail_copies = [tail_copy(i, ref) for i, ref in enumerate((k_ref, v_ref, q_ref))]
    for copy in tail_copies:
        copy.start()

    def exchange(source, target, send_sem, recv_sem):
        def to(peer):
            return pltpu.make_async_remote_copy(
                src_ref=source.at[at(peer), :],
                dst_ref=target.at[at(me), :],
                send_sem=send_sem.at[peer],
                recv_sem=recv_sem.at[me],
                device_id=(peer, core),
                device_id_type=MESH,
            )

        def come(peer):
            return pltpu.make_async_remote_copy(
                src_ref=source.at[at(peer), :],
                dst_ref=target.at[at(peer), :],
                send_sem=send_sem.at[peer],
                recv_sem=recv_sem.at[peer],
                device_id=(peer, core),
                device_id_type=MESH,
            )

        def start(j, carry):
            to(partner(j)).start()
            return carry

        def arrive(j, carry):
            come(partner(n - 2 - j)).wait_recv()
            return carry

        def leave(j, carry):
            to(partner(j)).wait_send()
            return carry

        return (
            lambda: lax.fori_loop(0, n - 1, start, 0),
            lambda: lax.fori_loop(0, n - 1, arrive, 0),
            lambda: lax.fori_loop(0, n - 1, leave, 0),
            come,
        )

    start_f, arrive_f, leave_f, _ = exchange(send_f, recv_f, f_send, f_recv)
    start_g, arrive_g, leave_g, _ = exchange(send_g, recv_g, g_send, g_recv)
    start_y, _, leave_y, come_y = exchange(send_y, recv_y, y_send, y_recv)
    start_f()
    for load in loads[6:]:
        load.start()

    first = me == 0

    def featured(stream, tail, ref, j):
        columns = lanes(j)
        before = tails[tail, :, columns].astype(jnp.float32)
        before = jnp.where(first, 0.0, before)
        window = jnp.concatenate([before, ref[:, columns].astype(jnp.float32)])
        total = feat_ref[stream, 0:1, columns] * window[16:]
        for tap in (1, 2):
            moved = pltpu.roll(window, tap, 0)[16:]
            total = total + feat_ref[stream, tap : tap + 1, columns] * moved
        return total

    for copy in tail_copies[:2]:
        copy.wait()

    def gate(j, carry):
        value = featured(1, 0, k_ref, j) * featured(2, 1, v_ref, j)
        gated[at(j), :] = value
        send_g[at(j), :] = value.astype(jnp.bfloat16)
        return carry

    lax.fori_loop(0, n, gate, 0)
    start_g()
    recv_g[at(me), :] = send_g[at(me), :]
    tail_copies[2].wait()

    def ask(j, carry):
        query[at(j), :] = featured(0, 2, q_ref, j)
        return carry

    lax.fori_loop(0, n, ask, 0)

    def block_of(ref):
        def load(block, start):
            where = pl.ds(pl.multiple_of(block * inner + start, CHUNK), CHUNK)
            return ref[where, :].astype(jnp.float32)

        return load

    def store(block, start, value):
        send_y[pl.ds(pl.multiple_of(block * inner + start, CHUNK), CHUNK), :] = value

    for load in loads[6:]:
        load.wait()
    arrive_f()
    spread_blocks(inner, block_of(recv_f), y_full, y_real, (low_full, low_real))
    filter_spectrum(f_full, f_real, y_full, y_real, low_full, low_real, h_full, h_real)
    arrive_g()
    spread_blocks(inner, block_of(recv_g), y_full, y_real)
    filtered(inner, f_full, f_real, g_full, g_real, y_full, y_real, h_full, h_real)
    gather_blocks(inner, h_full, h_real, store)
    start_y()
    recv_y[at(me), :] = send_y[at(me), :]

    def out_copy(block):
        return pltpu.make_async_copy(
            query.at[at(block), :], mixed_hbm.at[:, lanes(block)], out_sem.at[block]
        )

    def mix(block):
        conv = recv_y[at(block), :].astype(jnp.float32)
        mixed = query[at(block), :] * (conv + skip_ref[:, lanes(block)] * gated[at(block), :])
        query[at(block), :] = mixed
        out_copy(block).start()
        return mixed * mixed

    def mix_next(j, carry):
        block = partner(n - 2 - j)
        come_y(block).wait_recv()
        return carry + mix(block)

    sums[...] = lax.fori_loop(0, n - 1, mix_next, mix(me))
    sum_copy = pltpu.make_async_remote_copy(
        src_ref=sums,
        dst_ref=other_sums,
        send_sem=sum_sem.at[0],
        recv_sem=sum_sem.at[1],
        device_id=(me, other),
        device_id_type=MESH,
    )
    sum_copy.start()
    leave_f()
    leave_g()
    leave_y()

    def written(j, carry):
        out_copy(j).wait()
        return carry

    lax.fori_loop(0, n, written, 0)
    sum_copy.wait()
    total = jnp.sum(sums[...] + other_sums[...], axis=1, keepdims=True)
    scale_ref[...] = jnp.broadcast_to(lax.rsqrt(total / D + 1e-05), scale_ref.shape)


def channel_shards(q_proj, k_proj, v_proj, feat_filter, long_filter, skip_bias, norm_gain):
    rows, channels = q_proj.shape
    n = lax.axis_size("seq")
    seq = rows * n
    inner = seq // HALF
    tables = [jnp.asarray(t) for t in dft_tables(seq)]
    narrow, wide = jnp.bfloat16, jnp.float32
    scratch = [pltpu.VMEM(feat_filter.shape, wide), pltpu.VMEM((1, channels), wide)]
    scratch += [pltpu.VMEM((rows, channels), narrow)] * 3 + [pltpu.VMEM((rows, channels), wide)]
    scratch += [pltpu.VMEM(t.shape, narrow) for t in tables]
    scratch += [pltpu.VMEM((3, 16, channels), narrow)]
    scratch += [pltpu.VMEM((seq, LANES), narrow)] * 6
    scratch += [pltpu.VMEM((seq, LANES), wide)] * 2
    scratch += [pltpu.VMEM((rows, LANES), wide)] * 2
    scratch += spectrum_scratch(inner)
    scratch += [pltpu.SemaphoreType.DMA((10,))]
    scratch += [pltpu.SemaphoreType.DMA((3,))] * 2
    scratch += [pltpu.SemaphoreType.DMA((n,))] * 6
    scratch += [pltpu.SemaphoreType.DMA((2,)), pltpu.SemaphoreType.DMA((n,))]
    away = pl.BlockSpec(memory_space=pl.ANY)
    mixed, scale = pl.pallas_call(
        functools.partial(mixer_kernel, n, inner),
        out_shape=(
            jax.ShapeDtypeStruct((rows, channels), wide),
            jax.ShapeDtypeStruct((rows, LANES), wide),
        ),
        in_specs=[away] * 10,
        out_specs=(away, pl.BlockSpec(memory_space=pltpu.VMEM)),
        scratch_shapes=scratch,
        compiler_params=pltpu.CompilerParams(
            collective_id=0, has_side_effects=True, vmem_limit_bytes=VMEM_BYTES
        ),
    )(
        q_proj, k_proj, v_proj, long_filter, *tables, feat_filter, skip_bias.reshape(1, -1)
    )
    normed = mixed * scale[:, :1] * norm_gain
    return (mixed.astype(narrow), normed.astype(narrow))


def solution(mesh):
    def layer(*arrays):
        rows, channels = arrays[0].shape
        n = mesh.shape["seq"]
        seq = rows * n
        whole_lanes = channels == LANES * n and n % 2 == 0 and mesh.shape["ch"] == 2
        if whole_lanes and rows % 16 == 0 and seq % (2 * HALF * CHUNK) == 0 and seq <= 2048:
            return channel_shards(*arrays)
        return shards(*arrays)

    return jax.shard_map(
        layer,
        mesh=mesh,
        in_specs=(
            P("seq", "ch"),
            P("seq", "ch"),
            P("seq", "ch"),
            P(None, None, "ch"),
            P("seq", "ch"),
            P("ch"),
            P("ch"),
        ),
        out_specs=(P("seq", "ch"), P("seq", "ch")),
        check_vma=False,
    )
```

```python
import functools
import math

import jax
import jax.numpy as jnp
import numpy as np
from jax import lax
from jax.experimental import pallas as pl
from jax.experimental.pallas import tpu as pltpu
from jax.sharding import PartitionSpec as P

D = 4096
RADIX = 16
HALF = RADIX // 2
LANES = 128
VMEM_BYTES = 62 * 2**20
MESH = pl.DeviceIdType.MESH


def dft_tables(seq):
    length = 2 * seq
    inner = length // RADIX
    tokens = np.arange(inner, dtype=np.int64)

    def waves(freq):
        angle = (freq[:, None] * tokens[None, :] % length) * (2.0 * math.pi / length)
        return np.cos(angle), np.sin(angle)

    full = []
    for k1 in range(1, HALF):
        c, s = waves(k1 + RADIX * np.arange(inner, dtype=np.int64))
        full.append(np.block([[c, s], [-s, c]]))
    real = []
    for k1 in (0, HALF):
        c, s = waves(k1 + RADIX * np.arange(inner // 2, dtype=np.int64))
        table = np.concatenate([c, -s])
        if k1 == 0:
            table[inner // 2] = np.cos(math.pi * tokens)
        real.append(table)

    def split(table):
        high = table.astype(jnp.bfloat16)
        low = (table - high.astype(np.float64)).astype(jnp.bfloat16)
        return np.concatenate([high, low], axis=-1)

    full, real = np.stack(full), np.stack(real)
    turn = lambda a: np.swapaxes(a, 1, 2)
    return split(full), split(real), turn(full).astype(jnp.bfloat16), turn(real).astype(jnp.bfloat16)


def turned(cr, ci, a):
    return (cr * a[0] - ci * a[1], cr * a[1] + ci * a[0])


def unit(power):
    angle = 2.0 * math.pi * power / RADIX
    return math.cos(angle), math.sin(angle)


def block_dft(x):
    s = math.sqrt(0.5)
    a = [x[n] + x[n + 4] for n in range(4)]
    b = [x[n] - x[n + 4] for n in range(4)]
    out = {}
    e, o = a[0] + a[2], a[1] + a[3]
    out[0], out[8] = e + o, e - o
    out[4] = (a[0] - a[2], a[3] - a[1])
    d, m = s * (b[1] - b[3]), s * (b[1] + b[3])
    out[2] = (b[0] + d, -b[2] - m)
    out[6] = (b[0] - d, b[2] - m)
    for first, sign in ((1, -1.0), (3, 1.0)):
        t = [(x[0], sign * x[4])]
        for n in range(1, 4):
            cr, ci = unit(-first * n)
            t.append(turned(cr, ci, (x[n], sign * x[n + 4])))
        er, ei = t[0][0] + t[2][0], t[0][1] + t[2][1]
        dr, di = t[0][0] - t[2][0], t[0][1] - t[2][1]
        fr, fi = t[1][0] + t[3][0], t[1][1] + t[3][1]
        gr, gi = t[1][0] - t[3][0], t[1][1] - t[3][1]
        out[first] = (er + fr, ei + fi)
        out[first + 4] = (dr + gi, di - gr)
    return out


def block_idft(u):
    s = math.sqrt(0.5)
    p, m = u[0] + u[8], u[0] - u[8]
    a = [p + u[4][0], m - u[4][1], p - u[4][0], m + u[4][1]]
    b = [
        u[2][0] + u[6][0],
        s * ((u[2][0] - u[2][1]) - (u[6][0] + u[6][1])),
        u[6][1] - u[2][1],
        s * ((u[6][0] - u[6][1]) - (u[2][0] + u[2][1])),
    ]
    out = [None] * HALF
    for n in range(4):
        low, high = a[n] + b[n], a[n] - b[n]
        for first, sign in ((1, -1.0), (3, 1.0)):
            v, w = u[first], u[first + 4]
            if n == 0:
                v = (v[0] + w[0], v[1] + w[1])
            elif n == 1:
                v = (v[0] - w[1], v[1] + w[0])
            elif n == 2:
                v = (v[0] - w[0], v[1] - w[1])
            else:
                v = (v[0] + w[1], v[1] - w[0])
            q = turned(*unit(first * n), v)
            low, high = low + q[0], high + sign * q[1]
        out[n], out[n + 4] = low, high
    return out


CHUNK = 16


def spread_blocks(inner, load, y_full, y_real, rest=None):
    def put(ref, low_ref, k, rows, value):
        high = value.astype(jnp.bfloat16)
        ref[k, rows, :] = high
        if low_ref is not None:
            low_ref[k, rows, :] = (value - high.astype(jnp.float32)).astype(jnp.bfloat16)

    low_full, low_real = rest or (None, None)

    def step(i, carry):
        start = pl.multiple_of(i * CHUNK, CHUNK)
        rows = pl.ds(start, CHUNK)
        out = block_dft([load(n, start) for n in range(HALF)])
        put(y_real, low_real, 0, rows, out[0])
        put(y_real, low_real, 1, rows, out[HALF])
        lower = pl.ds(pl.multiple_of(inner + start, CHUNK), CHUNK)
        for k in range(1, HALF):
            put(y_full, low_full, k - 1, rows, out[k][0])
            put(y_full, low_full, k - 1, lower, out[k][1])
        return carry

    lax.fori_loop(0, inner // CHUNK, step, 0)


def dot(table, values):
    return jnp.dot(table, values, preferred_element_type=jnp.float32)


def careful(table, values, low):
    half = table.shape[1] // 2
    first = dot(table[:, :half], values) + dot(table[:, half:], values)
    return first + dot(table[:, :half], low)


def filter_spectrum(f_full, f_real, y_full, y_real, low_full, low_real, h_full, h_real):
    for i in range(2):
        h_real[i] = careful(f_real[i], y_real[i], low_real[i])

    def step(k, carry):
        h_full[k] = careful(f_full[k], y_full[k], low_full[k])
        return carry

    lax.fori_loop(0, HALF - 1, step, 0)


def filtered(inner, f_full, f_real, g_full, g_real, y_full, y_real, h_full, h_real):
    length = inner * RADIX

    def product(a, b, size):
        ar, ai, br, bi = a[:size], a[size:], b[:size], b[size:]
        return ar * br - ai * bi, ar * bi + ai * br

    for i in range(2):
        half = inner // 2
        a, b = dot(f_real[i, :, :inner], y_real[i]), h_real[i]
        pr, pi = product(a, b, half)
        pr, pi = pr * (2.0 / length), pi * (2.0 / length)
        if i == 0:
            top = lax.broadcasted_iota(jnp.int32, pr.shape, 0) == 0
            pr = jnp.where(top, a[:half] * b[:half] * (1.0 / length), pr)
            pi = jnp.where(top, a[half:] * b[half:] * (1.0 / length), pi)
        z = jnp.concatenate([pr, pi]).astype(jnp.bfloat16)
        h_real[i] = dot(g_real[i], z)

    def step(k, carry):
        pr, pi = product(dot(f_full[k, :, : 2 * inner], y_full[k]), h_full[k], inner)
        z = (jnp.concatenate([pr, pi]) * (2.0 / length)).astype(jnp.bfloat16)
        h_full[k] = dot(g_full[k], z)
        return carry

    lax.fori_loop(0, HALF - 1, step, 0)


def gather_blocks(inner, h_full, h_real, store):
    def step(i, carry):
        start = pl.multiple_of(i * CHUNK, CHUNK)
        rows = pl.ds(start, CHUNK)
        lower = pl.ds(pl.multiple_of(inner + start, CHUNK), CHUNK)
        u = {0: h_real[0, rows, :], HALF: h_real[1, rows, :]}
        for k in range(1, HALF):
            u[k] = (h_full[k - 1, rows, :], h_full[k - 1, lower, :])
        for n, block in enumerate(block_idft(u)):
            store(n, start, block.astype(jnp.bfloat16))
        return carry

    lax.fori_loop(0, inner // CHUNK, step, 0)


def spectrum_scratch(inner):
    wide = (HALF - 1, 2 * inner, LANES)
    return [
        pltpu.VMEM(wide, jnp.bfloat16),
        pltpu.VMEM((2, inner, LANES), jnp.bfloat16),
        pltpu.VMEM(wide, jnp.bfloat16),
        pltpu.VMEM((2, inner, LANES), jnp.bfloat16),
        pltpu.VMEM(wide, jnp.float32),
        pltpu.VMEM((2, inner, LANES), jnp.float32),
    ]


highest_precision = lax.Precision.HIGHEST


def shifted(block, axis, distance):
    devices = range(lax.axis_size(axis))
    route = [(i - distance, i) for i in devices if i - distance in devices]
    return lax.ppermute(block, axis, route)


def for_sending(value):
    return jax.tree.map(lambda a: a.astype(jnp.bfloat16) if a.dtype == jnp.float32 else a, value)


def angle_table(count, left, right):
    product = left[:, None] * right[None, :] % count
    angle = product.astype(jnp.float32) * (2.0 * math.pi / count)
    return (jnp.cos(angle), jnp.sin(angle))


def contract(pattern, table, values):
    return jnp.einsum(pattern, table, values, precision=highest_precision)


def rotate(pattern, cos_table, sin_table, real_part, imag_part, turning):
    out_real = contract(pattern, cos_table, real_part) - turning * contract(
        pattern, sin_table, imag_part
    )
    out_imag = contract(pattern, cos_table, imag_part) + turning * contract(
        pattern, sin_table, real_part
    )
    return (out_real, out_imag)


def frequency_order(groups):
    return jnp.arange(2 * groups, dtype=jnp.int32)


def shards(q_proj, k_proj, v_proj, feat_filter, long_filter, skip_bias, norm_gain):
    rows = q_proj.shape[0]
    taps = feat_filter.shape[1]
    groups = lax.axis_size("seq")
    stacked = jnp.stack([q_proj, k_proj, v_proj])
    previous = shifted(stacked[:, rows - (taps - 1) :, :], "seq", 1)
    extended = jnp.concatenate([previous, stacked], axis=1)
    featured = jnp.zeros(stacked.shape, jnp.float32)
    for offset in range(taps):
        window = extended[:, taps - 1 - offset : taps - 1 - offset + rows, :]
        featured = featured + feat_filter[:, offset, None, :] * window.astype(jnp.float32)
    query = featured[0]
    gated = featured[1] * featured[2]
    device = lax.axis_index("seq")
    per_device = rows // groups
    length = 2 * rows * groups
    order = frequency_order(groups)
    blocks = jnp.arange(groups, dtype=jnp.int32)
    within = jnp.arange(rows, dtype=jnp.int32)
    local_rows = device * per_device + jnp.arange(per_device, dtype=jnp.int32)
    slots = lax.dynamic_slice_in_dim(order, 2 * device, 2)
    cos_a, sin_a = angle_table(2 * groups, order, blocks)
    cos_w, sin_w = angle_table(length, order, local_rows)
    cos_b, sin_b = angle_table(rows, within, within)
    cos_v, sin_v = angle_table(length, slots, within)
    cos_i, sin_i = angle_table(2 * groups, blocks, order)
    signals = jnp.stack([gated, long_filter])[:, None]
    pieces = lax.all_to_all(
        signals.astype(jnp.bfloat16), "seq", split_axis=2, concat_axis=1, tiled=True
    ).astype(signals.dtype)
    real_part = contract("ka,xabc->xkbc", cos_a, pieces)
    imag_part = -contract("ka,xabc->xkbc", sin_a, pieces)
    cosine = cos_w[:, :, None]
    sine = sin_w[:, :, None]
    real_part, imag_part = (
        real_part * cosine + imag_part * sine,
        imag_part * cosine - real_part * sine,
    )
    spread = jnp.stack([real_part, imag_part], axis=1)
    pieces = lax.all_to_all(
        for_sending(spread), "seq", split_axis=2, concat_axis=3, tiled=True
    ).astype(spread.dtype)
    real_part, imag_part = rotate("kb,xsbc->xskc", cos_b, sin_b, pieces[:, 0], pieces[:, 1], -1.0)
    prod_real = real_part[0] * real_part[1] - imag_part[0] * imag_part[1]
    prod_imag = real_part[0] * imag_part[1] + imag_part[0] * real_part[1]
    real_part = prod_real
    imag_part = prod_imag
    real_part, imag_part = rotate("bk,skc->sbc", cos_b, sin_b, real_part, imag_part, 1.0)
    cosine = cos_v[:, :, None]
    sine = sin_v[:, :, None]
    spectra = jnp.stack(
        [real_part * cosine - imag_part * sine, imag_part * cosine + real_part * sine]
    )
    pieces = lax.all_to_all(
        for_sending(spectra), "seq", split_axis=2, concat_axis=1, tiled=True
    ).astype(spectra.dtype)
    summed = contract("ak,kbc->abc", cos_i, pieces[0]) - contract("ak,kbc->abc", sin_i, pieces[1])
    returned = summed / length
    long_conv = lax.all_to_all(
        for_sending(returned), "seq", split_axis=0, concat_axis=1, tiled=True
    ).astype(returned.dtype)[0]
    mixed = query * (long_conv + skip_bias * gated)
    squares = lax.psum(jnp.sum(mixed * mixed, axis=1), "ch")
    scale = lax.rsqrt(squares / D + 1e-05)
    normed = (mixed * scale[:, None] * norm_gain).astype(jnp.bfloat16)
    return (mixed.astype(jnp.bfloat16), normed)


def mixer_kernel(
    n, inner,
    q_hbm, k_hbm, v_hbm, filter_hbm, f_full_hbm, f_real_hbm, g_full_hbm, g_real_hbm,
    feat_hbm, skip_hbm, gain_hbm,
    mixed_hbm, normed_hbm,
    feat_ref, skip_ref, gain_ref, mixed_ref, normed_ref, q_ref, k_ref, v_ref, filter_ref, f_full, f_real, g_full, g_real,
    tails, send_f, send_g, send_y, recv_f, recv_g, recv_y, query, gated, sums, other_sums,
    y_full, y_real, low_full, low_real, h_full, h_real,
    local_sem, tail_send, tail_recv, f_send, f_recv, g_send, g_recv, y_send, y_recv, sum_sem, out_sem,
):
    me = lax.axis_index("seq")
    core = lax.axis_index("ch")
    other = 1 - core
    rows = q_ref.shape[0]
    after = lax.rem(me + 1, n)

    def at(block):
        return pl.ds(pl.multiple_of(block * rows, rows), rows)

    def lanes(block):
        return pl.ds(pl.multiple_of(block * LANES, LANES), LANES)

    def partner(j):
        quarter = n // 4
        offset = (3 - j % 4) * quarter + quarter - 1 - j // 4
        return lax.rem(me + offset, n)

    loads = [
        pltpu.make_async_copy(source, target, local_sem.at[i])
        for i, (source, target) in enumerate([
            (filter_hbm, filter_ref), (k_hbm, k_ref), (v_hbm, v_ref), (q_hbm, q_ref),
            (feat_hbm, feat_ref), (skip_hbm, skip_ref), (gain_hbm, gain_ref),
            (f_real_hbm, f_real), (f_full_hbm, f_full), (g_real_hbm, g_real), (g_full_hbm, g_full),
        ])
    ]
    for load in loads[:7]:
        load.start()

    barrier = pltpu.get_barrier_semaphore()

    def greet(j, carry):
        pl.semaphore_signal(
            barrier, inc=1, device_id=(partner(j), core), device_id_type=MESH
        )
        return carry

    lax.fori_loop(0, n - 1, greet, 0)
    pl.semaphore_signal(barrier, inc=1, device_id=(me, other), device_id_type=MESH)

    loads[0].wait()

    def narrow(j, carry):
        send_f[at(j), :] = filter_ref[:, lanes(j)].astype(jnp.bfloat16)
        return carry

    lax.fori_loop(0, n, narrow, 0)
    recv_f[at(me), :] = send_f[at(me), :]
    for load in loads[1:7]:
        load.wait()
    pl.semaphore_wait(barrier, n)

    def tail_copy(i, ref):
        return pltpu.make_async_remote_copy(
            src_ref=ref.at[pl.ds(rows - 16, 16), :],
            dst_ref=tails.at[i],
            send_sem=tail_send.at[i],
            recv_sem=tail_recv.at[i],
            device_id=(after, core),
            device_id_type=MESH,
        )

    tail_copies = [tail_copy(i, ref) for i, ref in enumerate((k_ref, v_ref, q_ref))]
    for copy in tail_copies:
        copy.start()

    def exchange(source, target, send_sem, recv_sem):
        def to(peer):
            return pltpu.make_async_remote_copy(
                src_ref=source.at[at(peer), :],
                dst_ref=target.at[at(me), :],
                send_sem=send_sem.at[peer],
                recv_sem=recv_sem.at[me],
                device_id=(peer, core),
                device_id_type=MESH,
            )

        def come(peer):
            return pltpu.make_async_remote_copy(
                src_ref=source.at[at(peer), :],
                dst_ref=target.at[at(peer), :],
                send_sem=send_sem.at[peer],
                recv_sem=recv_sem.at[peer],
                device_id=(peer, core),
                device_id_type=MESH,
            )

        def start(j, carry):
            to(partner(j)).start()
            return carry

        def arrive(j, carry):
            come(partner(n - 2 - j)).wait_recv()
            return carry

        def leave(j, carry):
            to(partner(j)).wait_send()
            return carry

        return (
            lambda: lax.fori_loop(0, n - 1, start, 0),
            lambda: lax.fori_loop(0, n - 1, arrive, 0),
            lambda: lax.fori_loop(0, n - 1, leave, 0),
            come,
        )

    start_f, arrive_f, leave_f, _ = exchange(send_f, recv_f, f_send, f_recv)
    start_g, arrive_g, leave_g, _ = exchange(send_g, recv_g, g_send, g_recv)
    start_y, _, leave_y, come_y = exchange(send_y, recv_y, y_send, y_recv)
    start_f()
    for load in loads[7:]:
        load.start()

    first = me == 0

    def featured(stream, tail, ref, j):
        columns = lanes(j)
        before = tails[tail, :, columns].astype(jnp.float32)
        before = jnp.where(first, 0.0, before)
        window = jnp.concatenate([before, ref[:, columns].astype(jnp.float32)])
        total = feat_ref[stream, 0:1, columns] * window[16:]
        for tap in (1, 2):
            moved = pltpu.roll(window, tap, 0)[16:]
            total = total + feat_ref[stream, tap : tap + 1, columns] * moved
        return total

    for copy in tail_copies[:2]:
        copy.wait()

    def gate(j, carry):
        value = featured(1, 0, k_ref, j) * featured(2, 1, v_ref, j)
        gated[at(j), :] = value
        send_g[at(j), :] = value.astype(jnp.bfloat16)
        return carry

    lax.fori_loop(0, n, gate, 0)
    start_g()
    recv_g[at(me), :] = send_g[at(me), :]
    tail_copies[2].wait()

    def ask(j, carry):
        query[at(j), :] = featured(0, 2, q_ref, j)
        return carry

    lax.fori_loop(0, n, ask, 0)

    def block_of(ref):
        def load(block, start):
            where = pl.ds(pl.multiple_of(block * inner + start, CHUNK), CHUNK)
            return ref[where, :].astype(jnp.float32)

        return load

    def store(block, start, value):
        send_y[pl.ds(pl.multiple_of(block * inner + start, CHUNK), CHUNK), :] = value

    for load in loads[7:]:
        load.wait()
    arrive_f()
    spread_blocks(inner, block_of(recv_f), y_full, y_real, (low_full, low_real))
    filter_spectrum(f_full, f_real, y_full, y_real, low_full, low_real, h_full, h_real)
    arrive_g()
    spread_blocks(inner, block_of(recv_g), y_full, y_real)
    filtered(inner, f_full, f_real, g_full, g_real, y_full, y_real, h_full, h_real)
    gather_blocks(inner, h_full, h_real, store)
    start_y()
    recv_y[at(me), :] = send_y[at(me), :]

    mixed_copy = pltpu.make_async_copy(mixed_ref, mixed_hbm, out_sem.at[0])
    normed_copy = pltpu.make_async_copy(normed_ref, normed_hbm, out_sem.at[1])

    def mix(block):
        conv = recv_y[at(block), :].astype(jnp.float32)
        mixed = query[at(block), :] * (conv + skip_ref[:, lanes(block)] * gated[at(block), :])
        query[at(block), :] = mixed
        mixed_ref[:, lanes(block)] = mixed.astype(jnp.bfloat16)
        return mixed * mixed

    def mix_next(j, carry):
        block = partner(n - 2 - j)
        come_y(block).wait_recv()
        return carry + mix(block)

    sums[...] = lax.fori_loop(0, n - 1, mix_next, mix(me))
    sum_copy = pltpu.make_async_remote_copy(
        src_ref=sums,
        dst_ref=other_sums,
        send_sem=sum_sem.at[0],
        recv_sem=sum_sem.at[1],
        device_id=(me, other),
        device_id_type=MESH,
    )
    sum_copy.start()
    mixed_copy.start()
    leave_f()
    leave_g()
    leave_y()
    sum_copy.wait()
    total = jnp.sum(sums[...] + other_sums[...], axis=1, keepdims=True)
    scale = lax.rsqrt(total / D + 1e-05)

    def norm(j, carry):
        value = query[at(j), :] * scale * gain_ref[:, lanes(j)]
        normed_ref[:, lanes(j)] = value.astype(jnp.bfloat16)
        return carry

    lax.fori_loop(0, n, norm, 0)
    normed_copy.start()
    mixed_copy.wait()
    normed_copy.wait()


def channel_shards(q_proj, k_proj, v_proj, feat_filter, long_filter, skip_bias, norm_gain):
    rows, channels = q_proj.shape
    n = lax.axis_size("seq")
    seq = rows * n
    inner = seq // HALF
    tables = [jnp.asarray(t) for t in dft_tables(seq)]
    narrow, wide = jnp.bfloat16, jnp.float32
    scratch = [pltpu.VMEM(feat_filter.shape, wide), pltpu.VMEM((1, channels), wide)]
    scratch += [pltpu.VMEM((1, channels), wide)] + [pltpu.VMEM((rows, channels), narrow)] * 2
    scratch += [pltpu.VMEM((rows, channels), narrow)] * 3 + [pltpu.VMEM((rows, channels), wide)]
    scratch += [pltpu.VMEM(t.shape, narrow) for t in tables]
    scratch += [pltpu.VMEM((3, 16, channels), narrow)]
    scratch += [pltpu.VMEM((seq, LANES), narrow)] * 6
    scratch += [pltpu.VMEM((seq, LANES), wide)] * 2
    scratch += [pltpu.VMEM((rows, LANES), wide)] * 2
    scratch += spectrum_scratch(inner)
    scratch += [pltpu.SemaphoreType.DMA((11,))]
    scratch += [pltpu.SemaphoreType.DMA((3,))] * 2
    scratch += [pltpu.SemaphoreType.DMA((n,))] * 6
    scratch += [pltpu.SemaphoreType.DMA((2,))] * 2
    away = pl.BlockSpec(memory_space=pl.ANY)
    out = jax.ShapeDtypeStruct((rows, channels), narrow)
    return tuple(pl.pallas_call(
        functools.partial(mixer_kernel, n, inner),
        out_shape=(out, out),
        in_specs=[away] * 11,
        out_specs=(away, away),
        scratch_shapes=scratch,
        compiler_params=pltpu.CompilerParams(
            collective_id=0, has_side_effects=True, vmem_limit_bytes=VMEM_BYTES
        ),
    )(
        q_proj, k_proj, v_proj, long_filter, *tables,
        feat_filter, skip_bias.reshape(1, -1), norm_gain.reshape(1, -1),
    ))


def solution(mesh):
    def layer(*arrays):
        rows, channels = arrays[0].shape
        n = mesh.shape["seq"]
        seq = rows * n
        whole_lanes = channels == LANES * n and n % 4 == 0 and mesh.shape["ch"] == 2
        if whole_lanes and rows % 16 == 0 and seq % (2 * HALF * CHUNK) == 0 and seq <= 2048:
            return channel_shards(*arrays)
        return shards(*arrays)

    return jax.shard_map(
        layer,
        mesh=mesh,
        in_specs=(
            P("seq", "ch"),
            P("seq", "ch"),
            P("seq", "ch"),
            P(None, None, "ch"),
            P("seq", "ch"),
            P("ch"),
            P("ch"),
        ),
        out_specs=(P("seq", "ch"), P("seq", "ch")),
        check_vma=False,
    )
```

```python
import functools
import math

import jax
import jax.numpy as jnp
import numpy as np
from jax import lax
from jax.experimental import pallas as pl
from jax.experimental.pallas import tpu as pltpu
from jax.sharding import PartitionSpec as P

D = 4096
RADIX = 16
HALF = RADIX // 2
LANES = 128
VMEM_BYTES = 48 * 2**20
MESH = pl.DeviceIdType.MESH


def dft_tables(seq):
    length = 2 * seq
    inner = length // RADIX
    tokens = np.arange(inner, dtype=np.int64)

    def waves(freq):
        angle = (freq[:, None] * tokens[None, :] % length) * (2.0 * math.pi / length)
        return np.cos(angle), np.sin(angle)

    full = []
    for k1 in range(1, HALF):
        c, s = waves(k1 + RADIX * np.arange(inner, dtype=np.int64))
        full.append(np.block([[c, s], [-s, c]]))
    real = []
    for k1 in (0, HALF):
        c, s = waves(k1 + RADIX * np.arange(inner // 2, dtype=np.int64))
        table = np.concatenate([c, -s])
        if k1 == 0:
            table[inner // 2] = np.cos(math.pi * tokens)
        real.append(table)

    def split(table):
        high = table.astype(jnp.bfloat16)
        low = (table - high.astype(np.float64)).astype(jnp.bfloat16)
        return np.concatenate([high, low], axis=-1)

    full, real = np.stack(full), np.stack(real)
    turn = lambda a: np.swapaxes(a, 1, 2)
    return split(full), split(real), turn(full).astype(jnp.bfloat16), turn(real).astype(jnp.bfloat16)


def turned(cr, ci, a):
    return (cr * a[0] - ci * a[1], cr * a[1] + ci * a[0])


def unit(power):
    angle = 2.0 * math.pi * power / RADIX
    return math.cos(angle), math.sin(angle)


def block_dft(x):
    s = math.sqrt(0.5)
    a = [x[n] + x[n + 4] for n in range(4)]
    b = [x[n] - x[n + 4] for n in range(4)]
    out = {}
    e, o = a[0] + a[2], a[1] + a[3]
    out[0], out[8] = e + o, e - o
    out[4] = (a[0] - a[2], a[3] - a[1])
    d, m = s * (b[1] - b[3]), s * (b[1] + b[3])
    out[2] = (b[0] + d, -b[2] - m)
    out[6] = (b[0] - d, b[2] - m)
    for first, sign in ((1, -1.0), (3, 1.0)):
        t = [(x[0], sign * x[4])]
        for n in range(1, 4):
            cr, ci = unit(-first * n)
            t.append(turned(cr, ci, (x[n], sign * x[n + 4])))
        er, ei = t[0][0] + t[2][0], t[0][1] + t[2][1]
        dr, di = t[0][0] - t[2][0], t[0][1] - t[2][1]
        fr, fi = t[1][0] + t[3][0], t[1][1] + t[3][1]
        gr, gi = t[1][0] - t[3][0], t[1][1] - t[3][1]
        out[first] = (er + fr, ei + fi)
        out[first + 4] = (dr + gi, di - gr)
    return out


def block_idft(u):
    s = math.sqrt(0.5)
    p, m = u[0] + u[8], u[0] - u[8]
    a = [p + u[4][0], m - u[4][1], p - u[4][0], m + u[4][1]]
    b = [
        u[2][0] + u[6][0],
        s * ((u[2][0] - u[2][1]) - (u[6][0] + u[6][1])),
        u[6][1] - u[2][1],
        s * ((u[6][0] - u[6][1]) - (u[2][0] + u[2][1])),
    ]
    out = [None] * HALF
    for n in range(4):
        low, high = a[n] + b[n], a[n] - b[n]
        for first, sign in ((1, -1.0), (3, 1.0)):
            v, w = u[first], u[first + 4]
            if n == 0:
                v = (v[0] + w[0], v[1] + w[1])
            elif n == 1:
                v = (v[0] - w[1], v[1] + w[0])
            elif n == 2:
                v = (v[0] - w[0], v[1] - w[1])
            else:
                v = (v[0] + w[1], v[1] - w[0])
            q = turned(*unit(first * n), v)
            low, high = low + q[0], high + sign * q[1]
        out[n], out[n + 4] = low, high
    return out


CHUNK = 16


def spread_blocks(inner, part, load, y_full, y_real, rest=None):
    def put(ref, low_ref, k, rows, value):
        high = value.astype(jnp.bfloat16)
        ref[k, rows, :] = high
        if low_ref is not None:
            low_ref[k, rows, :] = (value - high.astype(jnp.float32)).astype(jnp.bfloat16)

    low_full, low_real = rest or (None, None)

    def step(first, i, carry):
        offset = pl.multiple_of(i * CHUNK, CHUNK)
        start = pl.multiple_of(first + offset, CHUNK)
        rows = pl.ds(start, CHUNK)
        out = block_dft([load(n, first, offset) for n in range(HALF)])
        put(y_real, low_real, 0, rows, out[0])
        put(y_real, low_real, 1, rows, out[HALF])
        lower = pl.ds(pl.multiple_of(inner + start, CHUNK), CHUNK)
        for k in range(1, HALF):
            put(y_full, low_full, k - 1, rows, out[k][0])
            put(y_full, low_full, k - 1, lower, out[k][1])
        return carry

    for first in range(0, inner, part):
        lax.fori_loop(0, part // CHUNK, functools.partial(step, first), 0)


def dot(table, values):
    return jnp.dot(table, values, preferred_element_type=jnp.float32)


def careful(table, values, low):
    half = table.shape[1] // 2
    first = dot(table[:, :half], values) + dot(table[:, half:], values)
    return first + dot(table[:, :half], low)


def filter_spectrum(f_full, f_real, y_full, y_real, low_full, low_real, h_full, h_real):
    for i in range(2):
        h_real[i] = careful(f_real[i], y_real[i], low_real[i])

    def step(k, carry):
        h_full[k] = careful(f_full[k], y_full[k], low_full[k])
        return carry

    lax.fori_loop(0, HALF - 1, step, 0)


def filtered(inner, f_full, f_real, g_full, g_real, y_full, y_real, h_full, h_real, z_full, z_real):
    length = inner * RADIX

    def product(a, b, size):
        ar, ai, br, bi = a[:size], a[size:], b[:size], b[size:]
        return ar * br - ai * bi, ar * bi + ai * br

    for i in range(2):
        half = inner // 2
        a, b = dot(f_real[i, :, :inner], y_real[i]), h_real[i]
        pr, pi = product(a, b, half)
        pr, pi = pr * (2.0 / length), pi * (2.0 / length)
        if i == 0:
            top = lax.broadcasted_iota(jnp.int32, pr.shape, 0) == 0
            pr = jnp.where(top, a[:half] * b[:half] * (1.0 / length), pr)
            pi = jnp.where(top, a[half:] * b[half:] * (1.0 / length), pi)
        z = jnp.concatenate([pr, pi]).astype(jnp.bfloat16)
        z_real[i] = dot(g_real[i], z)

    def step(k, carry):
        pr, pi = product(dot(f_full[k, :, : 2 * inner], y_full[k]), h_full[k], inner)
        z = (jnp.concatenate([pr, pi]) * (2.0 / length)).astype(jnp.bfloat16)
        z_full[k] = dot(g_full[k], z)
        return carry

    lax.fori_loop(0, HALF - 1, step, 0)


def gather_blocks(inner, part, h_full, h_real, store):
    def step(first, i, carry):
        offset = pl.multiple_of(i * CHUNK, CHUNK)
        start = pl.multiple_of(first + offset, CHUNK)
        rows = pl.ds(start, CHUNK)
        lower = pl.ds(pl.multiple_of(inner + start, CHUNK), CHUNK)
        u = {0: h_real[0, rows, :], HALF: h_real[1, rows, :]}
        for k in range(1, HALF):
            u[k] = (h_full[k - 1, rows, :], h_full[k - 1, lower, :])
        for n, block in enumerate(block_idft(u)):
            store(n, first, offset, block)
        return carry

    for first in range(0, inner, part):
        lax.fori_loop(0, part // CHUNK, functools.partial(step, first), 0)


def spectrum_scratch(inner):
    wide = (HALF - 1, 2 * inner, LANES)
    return [
        pltpu.VMEM(wide, jnp.bfloat16),
        pltpu.VMEM((2, inner, LANES), jnp.bfloat16),
        pltpu.VMEM(wide, jnp.bfloat16),
        pltpu.VMEM((2, inner, LANES), jnp.bfloat16),
        pltpu.VMEM(wide, jnp.float32),
        pltpu.VMEM((2, inner, LANES), jnp.float32),
        pltpu.VMEM(wide, jnp.float32),
        pltpu.VMEM((2, inner, LANES), jnp.float32),
    ]


highest_precision = lax.Precision.HIGHEST


def shifted(block, axis, distance):
    devices = range(lax.axis_size(axis))
    route = [(i - distance, i) for i in devices if i - distance in devices]
    return lax.ppermute(block, axis, route)


def for_sending(value):
    return jax.tree.map(lambda a: a.astype(jnp.bfloat16) if a.dtype == jnp.float32 else a, value)


def angle_table(count, left, right):
    product = left[:, None] * right[None, :] % count
    angle = product.astype(jnp.float32) * (2.0 * math.pi / count)
    return (jnp.cos(angle), jnp.sin(angle))


def contract(pattern, table, values):
    return jnp.einsum(pattern, table, values, precision=highest_precision)


def rotate(pattern, cos_table, sin_table, real_part, imag_part, turning):
    out_real = contract(pattern, cos_table, real_part) - turning * contract(
        pattern, sin_table, imag_part
    )
    out_imag = contract(pattern, cos_table, imag_part) + turning * contract(
        pattern, sin_table, real_part
    )
    return (out_real, out_imag)


def frequency_order(groups):
    return jnp.arange(2 * groups, dtype=jnp.int32)


def shards(q_proj, k_proj, v_proj, feat_filter, long_filter, skip_bias, norm_gain):
    rows = q_proj.shape[0]
    taps = feat_filter.shape[1]
    groups = lax.axis_size("seq")
    stacked = jnp.stack([q_proj, k_proj, v_proj])
    previous = shifted(stacked[:, rows - (taps - 1) :, :], "seq", 1)
    extended = jnp.concatenate([previous, stacked], axis=1)
    featured = jnp.zeros(stacked.shape, jnp.float32)
    for offset in range(taps):
        window = extended[:, taps - 1 - offset : taps - 1 - offset + rows, :]
        featured = featured + feat_filter[:, offset, None, :] * window.astype(jnp.float32)
    query = featured[0]
    gated = featured[1] * featured[2]
    device = lax.axis_index("seq")
    per_device = rows // groups
    length = 2 * rows * groups
    order = frequency_order(groups)
    blocks = jnp.arange(groups, dtype=jnp.int32)
    within = jnp.arange(rows, dtype=jnp.int32)
    local_rows = device * per_device + jnp.arange(per_device, dtype=jnp.int32)
    slots = lax.dynamic_slice_in_dim(order, 2 * device, 2)
    cos_a, sin_a = angle_table(2 * groups, order, blocks)
    cos_w, sin_w = angle_table(length, order, local_rows)
    cos_b, sin_b = angle_table(rows, within, within)
    cos_v, sin_v = angle_table(length, slots, within)
    cos_i, sin_i = angle_table(2 * groups, blocks, order)
    signals = jnp.stack([gated, long_filter])[:, None]
    pieces = lax.all_to_all(
        signals.astype(jnp.bfloat16), "seq", split_axis=2, concat_axis=1, tiled=True
    ).astype(signals.dtype)
    real_part = contract("ka,xabc->xkbc", cos_a, pieces)
    imag_part = -contract("ka,xabc->xkbc", sin_a, pieces)
    cosine = cos_w[:, :, None]
    sine = sin_w[:, :, None]
    real_part, imag_part = (
        real_part * cosine + imag_part * sine,
        imag_part * cosine - real_part * sine,
    )
    spread = jnp.stack([real_part, imag_part], axis=1)
    pieces = lax.all_to_all(
        for_sending(spread), "seq", split_axis=2, concat_axis=3, tiled=True
    ).astype(spread.dtype)
    real_part, imag_part = rotate("kb,xsbc->xskc", cos_b, sin_b, pieces[:, 0], pieces[:, 1], -1.0)
    prod_real = real_part[0] * real_part[1] - imag_part[0] * imag_part[1]
    prod_imag = real_part[0] * imag_part[1] + imag_part[0] * real_part[1]
    real_part = prod_real
    imag_part = prod_imag
    real_part, imag_part = rotate("bk,skc->sbc", cos_b, sin_b, real_part, imag_part, 1.0)
    cosine = cos_v[:, :, None]
    sine = sin_v[:, :, None]
    spectra = jnp.stack(
        [real_part * cosine - imag_part * sine, imag_part * cosine + real_part * sine]
    )
    pieces = lax.all_to_all(
        for_sending(spectra), "seq", split_axis=2, concat_axis=1, tiled=True
    ).astype(spectra.dtype)
    summed = contract("ak,kbc->abc", cos_i, pieces[0]) - contract("ak,kbc->abc", sin_i, pieces[1])
    returned = summed / length
    long_conv = lax.all_to_all(
        for_sending(returned), "seq", split_axis=0, concat_axis=1, tiled=True
    ).astype(returned.dtype)[0]
    mixed = query * (long_conv + skip_bias * gated)
    squares = lax.psum(jnp.sum(mixed * mixed, axis=1), "ch")
    scale = lax.rsqrt(squares / D + 1e-05)
    normed = (mixed * scale[:, None] * norm_gain).astype(jnp.bfloat16)
    return (mixed.astype(jnp.bfloat16), normed)


def mixer_kernel(
    n, inner,
    q_hbm, k_hbm, v_hbm, filter_hbm, f_full_hbm, f_real_hbm, g_full_hbm, g_real_hbm,
    feat_hbm, skip_hbm, gain_hbm,
    mixed_ref, normed_ref,
    feat_ref, skip_ref, gain_ref, q_ref, k_ref, v_ref, filter_ref, f_full, f_real, g_full, g_real,
    tails, send_f, recv_f, send_a, send_b, recv_a, recv_b,
    send_ya, send_yb, recv_ya, recv_yb, query, gated, sums, other_sums,
    y_full, y_real, low_full, low_real, h_full, h_real, z_full, z_real,
    local_sem, tail_send, tail_recv, f_send, f_recv, a_send, a_recv, b_send, b_recv,
    ya_send, ya_recv, yb_send, yb_recv, sum_sem,
):
    me = lax.axis_index("seq")
    core = lax.axis_index("ch")
    other = 1 - core
    rows = q_ref.shape[0]
    after = lax.rem(me + 1, n)

    def at(block):
        return pl.ds(pl.multiple_of(block * rows, rows), rows)

    part = rows // 2

    def packed_at(block):
        return pl.ds(pl.multiple_of(block * part, part), part)

    def swap(value):
        return pltpu.roll(value, LANES // 2, 1)

    lower = lax.broadcasted_iota(jnp.int32, (part, LANES), 1) < LANES // 2

    def lanes(block):
        return pl.ds(pl.multiple_of(block * LANES, LANES), LANES)

    def partner(j):
        offset = n // 2 + ((j + 1) // 2) * (2 * (j % 2) - 1)
        return lax.rem(me + offset, n)

    loads = [
        pltpu.make_async_copy(source, target, local_sem.at[i])
        for i, (source, target) in enumerate([
            (filter_hbm, filter_ref), (k_hbm, k_ref), (v_hbm, v_ref), (q_hbm, q_ref),
            (feat_hbm, feat_ref), (skip_hbm, skip_ref), (gain_hbm, gain_ref),
            (f_real_hbm, f_real), (f_full_hbm, f_full), (g_real_hbm, g_real), (g_full_hbm, g_full),
        ])
    ]
    for load in loads[:7]:
        load.start()

    barrier = pltpu.get_barrier_semaphore()

    def greet(j, carry):
        pl.semaphore_signal(
            barrier, inc=1, device_id=(partner(j), core), device_id_type=MESH
        )
        return carry

    lax.fori_loop(0, n - 1, greet, 0)
    pl.semaphore_signal(barrier, inc=1, device_id=(me, other), device_id_type=MESH)

    loads[0].wait()

    def narrow(j, carry):
        send_f[at(j), :] = filter_ref[:, lanes(j)].astype(jnp.bfloat16)
        return carry

    lax.fori_loop(0, n, narrow, 0)
    recv_f[at(me), :] = send_f[at(me), :]
    for load in loads[1:7]:
        load.wait()
    pl.semaphore_wait(barrier, n)

    def tail_copy(i, ref):
        return pltpu.make_async_remote_copy(
            src_ref=ref.at[pl.ds(rows - 16, 16), :],
            dst_ref=tails.at[i],
            send_sem=tail_send.at[i],
            recv_sem=tail_recv.at[i],
            device_id=(after, core),
            device_id_type=MESH,
        )

    tail_copies = [tail_copy(i, ref) for i, ref in enumerate((k_ref, v_ref, q_ref))]
    for copy in tail_copies:
        copy.start()

    def exchange(at, source, target, send_sem, recv_sem):
        def to(peer):
            return pltpu.make_async_remote_copy(
                src_ref=source.at[at(peer), :],
                dst_ref=target.at[at(me), :],
                send_sem=send_sem.at[peer],
                recv_sem=recv_sem.at[me],
                device_id=(peer, core),
                device_id_type=MESH,
            )

        def come(peer):
            return pltpu.make_async_remote_copy(
                src_ref=source.at[at(peer), :],
                dst_ref=target.at[at(peer), :],
                send_sem=send_sem.at[peer],
                recv_sem=recv_sem.at[peer],
                device_id=(peer, core),
                device_id_type=MESH,
            )

        def start(j, carry):
            to(partner(j)).start()
            return carry

        def arrive(j, carry):
            come(partner(n - 2 - j)).wait_recv()
            return carry

        def leave(j, carry):
            to(partner(j)).wait_send()
            return carry

        return (
            lambda: lax.fori_loop(0, n - 1, start, 0),
            lambda: lax.fori_loop(0, n - 1, arrive, 0),
            lambda: lax.fori_loop(0, n - 1, leave, 0),
            come,
        )

    start_f, arrive_f, leave_f, _ = exchange(at, send_f, recv_f, f_send, f_recv)
    start_a, arrive_a, leave_a, _ = exchange(packed_at, send_a, recv_a, a_send, a_recv)
    start_b, arrive_b, leave_b, _ = exchange(packed_at, send_b, recv_b, b_send, b_recv)
    start_ya, _, leave_ya, come_ya = exchange(packed_at, send_ya, recv_ya, ya_send, ya_recv)
    start_yb, _, leave_yb, come_yb = exchange(packed_at, send_yb, recv_yb, yb_send, yb_recv)
    start_f()
    for load in loads[7:]:
        load.start()

    first = me == 0

    def featured(stream, tail, ref, j):
        columns = lanes(j)
        before = tails[tail, :, columns].astype(jnp.float32)
        before = jnp.where(first, 0.0, before)
        window = jnp.concatenate([before, ref[:, columns].astype(jnp.float32)])
        total = feat_ref[stream, 0:1, columns] * window[16:]
        for tap in (1, 2):
            moved = pltpu.roll(window, tap, 0)[16:]
            total = total + feat_ref[stream, tap : tap + 1, columns] * moved
        return total

    for copy in tail_copies[:2]:
        copy.wait()

    def gate(j, carry):
        value = featured(1, 0, k_ref, j) * featured(2, 1, v_ref, j)
        gated[at(j), :] = value
        top, bottom = value[:part], value[part:]
        half_a = jnp.where(lower, top, swap(bottom))
        half_b = jnp.where(lower, swap(top), bottom)
        send_a[packed_at(j), :] = half_a.astype(jnp.bfloat16)
        send_b[packed_at(j), :] = half_b.astype(jnp.bfloat16)
        return carry

    lax.fori_loop(0, n, gate, 0)
    start_a()
    start_b()
    recv_a[packed_at(me), :] = send_a[packed_at(me), :]
    recv_b[packed_at(me), :] = send_b[packed_at(me), :]
    tail_copies[2].wait()

    def ask(j, carry):
        query[at(j), :] = featured(0, 2, q_ref, j)
        return carry

    lax.fori_loop(0, n, ask, 0)

    def load_filter(block, first, offset):
        where = pl.ds(pl.multiple_of(block * inner + first + offset, CHUNK), CHUNK)
        return recv_f[where, :].astype(jnp.float32)

    def place(block, first, offset):
        piece = (block * inner + first) // part
        start = piece // 2 * part + offset
        return pl.ds(pl.multiple_of(start, CHUNK), CHUNK), piece % 2

    def load_half(ref, own, block, first, offset):
        where, side = place(block, first, offset)
        value = ref[where, :].astype(jnp.float32)
        return value if side == own else swap(value)

    def store_half(ref, own, block, first, offset, value):
        where, side = place(block, first, offset)
        value = (value if side == own else swap(value)).astype(jnp.bfloat16)
        if side == 0:
            ref[where, :] = value
        else:
            ref[where, LANES // 2 :] = value[:, LANES // 2 :]

    def transform(source, target, own):
        load = functools.partial(load_half, source, own)
        spread_blocks(inner, part, load, y_full, y_real)
        filtered(
            inner, f_full, f_real, g_full, g_real, y_full, y_real, h_full, h_real, z_full, z_real
        )
        gather_blocks(inner, part, z_full, z_real, functools.partial(store_half, target, own))

    for load in loads[7:]:
        load.wait()
    arrive_f()
    spread_blocks(inner, part, load_filter, y_full, y_real, (low_full, low_real))
    filter_spectrum(f_full, f_real, y_full, y_real, low_full, low_real, h_full, h_real)
    arrive_a()
    transform(recv_a, send_ya, 0)
    start_ya()
    recv_ya[packed_at(me), :] = send_ya[packed_at(me), :]
    arrive_b()
    transform(recv_b, send_yb, 1)
    start_yb()
    recv_yb[packed_at(me), :] = send_yb[packed_at(me), :]

    def mix(block):
        half_a = recv_ya[packed_at(block), :].astype(jnp.float32)
        half_b = recv_yb[packed_at(block), :].astype(jnp.float32)
        top = jnp.where(lower, half_a, swap(half_b))
        bottom = jnp.where(lower, swap(half_a), half_b)
        conv = jnp.concatenate([top, bottom])
        mixed = query[at(block), :] * (conv + skip_ref[:, lanes(block)] * gated[at(block), :])
        query[at(block), :] = mixed
        mixed_ref[:, lanes(block)] = mixed.astype(jnp.bfloat16)
        return mixed * mixed

    def mix_next(j, carry):
        block = partner(n - 2 - j)
        come_ya(block).wait_recv()
        come_yb(block).wait_recv()
        return carry + mix(block)

    sums[...] = lax.fori_loop(0, n - 1, mix_next, mix(me))
    sum_copy = pltpu.make_async_remote_copy(
        src_ref=sums,
        dst_ref=other_sums,
        send_sem=sum_sem.at[0],
        recv_sem=sum_sem.at[1],
        device_id=(me, other),
        device_id_type=MESH,
    )
    sum_copy.start()
    for leave in (leave_f, leave_a, leave_b, leave_ya, leave_yb):
        leave()
    sum_copy.wait()
    total = jnp.sum(sums[...] + other_sums[...], axis=1, keepdims=True)
    scale = lax.rsqrt(total / D + 1e-05)

    def norm(j, carry):
        value = query[at(j), :] * scale * gain_ref[:, lanes(j)]
        normed_ref[:, lanes(j)] = value.astype(jnp.bfloat16)
        return carry

    lax.fori_loop(0, n, norm, 0)


def channel_shards(q_proj, k_proj, v_proj, feat_filter, long_filter, skip_bias, norm_gain):
    rows, channels = q_proj.shape
    n = lax.axis_size("seq")
    seq = rows * n
    inner = seq // HALF
    tables = [jnp.asarray(t) for t in dft_tables(seq)]
    narrow, wide = jnp.bfloat16, jnp.float32
    scratch = [pltpu.VMEM(feat_filter.shape, wide), pltpu.VMEM((1, channels), wide)]
    scratch += [pltpu.VMEM((1, channels), wide)]
    scratch += [pltpu.VMEM((rows, channels), narrow)] * 3 + [pltpu.VMEM((rows, channels), wide)]
    scratch += [pltpu.VMEM(t.shape, narrow) for t in tables]
    scratch += [pltpu.VMEM((3, 16, channels), narrow)]
    scratch += [pltpu.VMEM((seq, LANES), narrow)] * 2
    scratch += [pltpu.VMEM((seq // 2, LANES), narrow)] * 8
    scratch += [pltpu.VMEM((seq, LANES), wide)] * 2
    scratch += [pltpu.VMEM((rows, LANES), wide)] * 2
    scratch += spectrum_scratch(inner)
    scratch += [pltpu.SemaphoreType.DMA((11,))]
    scratch += [pltpu.SemaphoreType.DMA((3,))] * 2
    scratch += [pltpu.SemaphoreType.DMA((n,))] * 10
    scratch += [pltpu.SemaphoreType.DMA((2,))]
    away = pl.BlockSpec(memory_space=pltpu.HBM)
    whole = pl.BlockSpec(memory_space=pltpu.VMEM)
    out = jax.ShapeDtypeStruct((rows, channels), narrow)
    operands = [q_proj, k_proj, v_proj, long_filter, *tables, feat_filter]
    operands += [skip_bias.reshape(1, -1), norm_gain.reshape(1, -1)]
    return tuple(pl.pallas_call(
        functools.partial(mixer_kernel, n, inner),
        out_shape=(out, out),
        in_specs=[away] * 11,
        out_specs=(whole, whole),
        scratch_shapes=scratch,
        compiler_params=pltpu.CompilerParams(
            collective_id=0, has_side_effects=True, vmem_limit_bytes=VMEM_BYTES
        ),
    )(*[pltpu.with_memory_space_constraint(a, pltpu.HBM) for a in operands]))


def solution(mesh):
    def layer(*arrays):
        rows, channels = arrays[0].shape
        n = mesh.shape["seq"]
        seq = rows * n
        whole_lanes = channels == LANES * n and n % 4 == 0 and rows % 64 == 0 and mesh.shape["ch"] == 2
        if whole_lanes and seq % (2 * HALF * CHUNK) == 0 and seq <= 2048:
            return channel_shards(*arrays)
        return shards(*arrays)

    return jax.shard_map(
        layer,
        mesh=mesh,
        in_specs=(
            P("seq", "ch"),
            P("seq", "ch"),
            P("seq", "ch"),
            P(None, None, "ch"),
            P("seq", "ch"),
            P("ch"),
            P("ch"),
        ),
        out_specs=(P("seq", "ch"), P("seq", "ch")),
        check_vma=False,
    )
```

```python
import functools
import math

import jax
import jax.numpy as jnp
import numpy as np
from jax import lax
from jax.experimental import pallas as pl
from jax.experimental.pallas import tpu as pltpu
from jax.sharding import PartitionSpec as P

D = 4096
RADIX = 16
HALF = RADIX // 2
LANES = 128
VMEM_BYTES = 48 * 2**20
MESH = pl.DeviceIdType.MESH


def dft_tables(seq):
    length = 2 * seq
    inner = length // RADIX
    tokens = np.arange(inner, dtype=np.int64)

    def waves(freq):
        angle = (freq[:, None] * tokens[None, :] % length) * (2.0 * math.pi / length)
        return np.cos(angle), np.sin(angle)

    full = []
    for k1 in range(1, HALF):
        c, s = waves(k1 + RADIX * np.arange(inner, dtype=np.int64))
        full.append(np.block([[c, s], [-s, c]]))
    real = []
    for k1 in (0, HALF):
        c, s = waves(k1 + RADIX * np.arange(inner // 2, dtype=np.int64))
        table = np.concatenate([c, -s])
        if k1 == 0:
            table[inner // 2] = np.cos(math.pi * tokens)
        real.append(table)

    def split(table):
        high = table.astype(jnp.bfloat16)
        low = (table - high.astype(np.float64)).astype(jnp.bfloat16)
        return np.concatenate([high, low], axis=-1)

    full, real = np.stack(full), np.stack(real)
    turn = lambda a: np.swapaxes(a, 1, 2)
    return split(full), split(real), turn(full).astype(jnp.bfloat16), turn(real).astype(jnp.bfloat16)


def turned(cr, ci, a):
    return (cr * a[0] - ci * a[1], cr * a[1] + ci * a[0])


def unit(power):
    angle = 2.0 * math.pi * power / RADIX
    return math.cos(angle), math.sin(angle)


def block_dft(x):
    s = math.sqrt(0.5)
    a = [x[n] + x[n + 4] for n in range(4)]
    b = [x[n] - x[n + 4] for n in range(4)]
    out = {}
    e, o = a[0] + a[2], a[1] + a[3]
    out[0], out[8] = e + o, e - o
    out[4] = (a[0] - a[2], a[3] - a[1])
    d, m = s * (b[1] - b[3]), s * (b[1] + b[3])
    out[2] = (b[0] + d, -b[2] - m)
    out[6] = (b[0] - d, b[2] - m)
    for first, sign in ((1, -1.0), (3, 1.0)):
        t = [(x[0], sign * x[4])]
        for n in range(1, 4):
            cr, ci = unit(-first * n)
            t.append(turned(cr, ci, (x[n], sign * x[n + 4])))
        er, ei = t[0][0] + t[2][0], t[0][1] + t[2][1]
        dr, di = t[0][0] - t[2][0], t[0][1] - t[2][1]
        fr, fi = t[1][0] + t[3][0], t[1][1] + t[3][1]
        gr, gi = t[1][0] - t[3][0], t[1][1] - t[3][1]
        out[first] = (er + fr, ei + fi)
        out[first + 4] = (dr + gi, di - gr)
    return out


def block_idft(u):
    s = math.sqrt(0.5)
    p, m = u[0] + u[8], u[0] - u[8]
    a = [p + u[4][0], m - u[4][1], p - u[4][0], m + u[4][1]]
    b = [
        u[2][0] + u[6][0],
        s * ((u[2][0] - u[2][1]) - (u[6][0] + u[6][1])),
        u[6][1] - u[2][1],
        s * ((u[6][0] - u[6][1]) - (u[2][0] + u[2][1])),
    ]
    out = [None] * HALF
    for n in range(4):
        low, high = a[n] + b[n], a[n] - b[n]
        for first, sign in ((1, -1.0), (3, 1.0)):
            v, w = u[first], u[first + 4]
            if n == 0:
                v = (v[0] + w[0], v[1] + w[1])
            elif n == 1:
                v = (v[0] - w[1], v[1] + w[0])
            elif n == 2:
                v = (v[0] - w[0], v[1] - w[1])
            else:
                v = (v[0] + w[1], v[1] - w[0])
            q = turned(*unit(first * n), v)
            low, high = low + q[0], high + sign * q[1]
        out[n], out[n + 4] = low, high
    return out


CHUNK = 16


def spread_blocks(inner, load, y_full, y_real, rest=None):
    def put(ref, low_ref, k, rows, value):
        high = value.astype(jnp.bfloat16)
        ref[k, rows, :] = high
        if low_ref is not None:
            low_ref[k, rows, :] = (value - high.astype(jnp.float32)).astype(jnp.bfloat16)

    low_full, low_real = rest or (None, None)

    def step(i, carry):
        start = pl.multiple_of(i * CHUNK, CHUNK)
        rows = pl.ds(start, CHUNK)
        out = block_dft([load(n, start) for n in range(HALF)])
        put(y_real, low_real, 0, rows, out[0])
        put(y_real, low_real, 1, rows, out[HALF])
        lower = pl.ds(pl.multiple_of(inner + start, CHUNK), CHUNK)
        for k in range(1, HALF):
            put(y_full, low_full, k - 1, rows, out[k][0])
            put(y_full, low_full, k - 1, lower, out[k][1])
        return carry

    lax.fori_loop(0, inner // CHUNK, step, 0)


def dot(table, values):
    return jnp.dot(table, values, preferred_element_type=jnp.float32)


def careful(table, values, low):
    half = table.shape[1] // 2
    first = dot(table[:, :half], values) + dot(table[:, half:], values)
    return first + dot(table[:, :half], low)


def filter_spectrum(f_full, f_real, y_full, y_real, low_full, low_real, h_full, h_real):
    for i in range(2):
        h_real[i] = careful(f_real[i], y_real[i], low_real[i])

    def step(k, carry):
        h_full[k] = careful(f_full[k], y_full[k], low_full[k])
        return carry

    lax.fori_loop(0, HALF - 1, step, 0)


def filtered(inner, f_full, f_real, g_full, g_real, y_full, y_real, h_full, h_real):
    length = inner * RADIX

    def product(a, b, size):
        ar, ai, br, bi = a[:size], a[size:], b[:size], b[size:]
        return ar * br - ai * bi, ar * bi + ai * br

    for i in range(2):
        half = inner // 2
        a, b = dot(f_real[i, :, :inner], y_real[i]), h_real[i]
        pr, pi = product(a, b, half)
        pr, pi = pr * (2.0 / length), pi * (2.0 / length)
        if i == 0:
            top = lax.broadcasted_iota(jnp.int32, pr.shape, 0) == 0
            pr = jnp.where(top, a[:half] * b[:half] * (1.0 / length), pr)
            pi = jnp.where(top, a[half:] * b[half:] * (1.0 / length), pi)
        z = jnp.concatenate([pr, pi]).astype(jnp.bfloat16)
        h_real[i] = dot(g_real[i], z)

    ahead = dot(f_full[0, :, : 2 * inner], y_full[0])
    for k in range(HALF - 1):
        spectrum = ahead
        if k + 1 < HALF - 1:
            ahead = dot(f_full[k + 1, :, : 2 * inner], y_full[k + 1])
        pr, pi = product(spectrum, h_full[k], inner)
        z = (jnp.concatenate([pr, pi]) * (2.0 / length)).astype(jnp.bfloat16)
        h_full[k] = dot(g_full[k], z)


def gather_blocks(inner, h_full, h_real, store):
    def step(i, carry):
        start = pl.multiple_of(i * CHUNK, CHUNK)
        rows = pl.ds(start, CHUNK)
        lower = pl.ds(pl.multiple_of(inner + start, CHUNK), CHUNK)
        u = {0: h_real[0, rows, :], HALF: h_real[1, rows, :]}
        for k in range(1, HALF):
            u[k] = (h_full[k - 1, rows, :], h_full[k - 1, lower, :])
        for n, block in enumerate(block_idft(u)):
            store(n, start, block.astype(jnp.bfloat16))
        return carry

    lax.fori_loop(0, inner // CHUNK, step, 0)


def spectrum_scratch(inner):
    wide = (HALF - 1, 2 * inner, LANES)
    return [
        pltpu.VMEM(wide, jnp.bfloat16),
        pltpu.VMEM((2, inner, LANES), jnp.bfloat16),
        pltpu.VMEM(wide, jnp.bfloat16),
        pltpu.VMEM((2, inner, LANES), jnp.bfloat16),
        pltpu.VMEM(wide, jnp.float32),
        pltpu.VMEM((2, inner, LANES), jnp.float32),
    ]


highest_precision = lax.Precision.HIGHEST


def shifted(block, axis, distance):
    devices = range(lax.axis_size(axis))
    route = [(i - distance, i) for i in devices if i - distance in devices]
    return lax.ppermute(block, axis, route)


def for_sending(value):
    return jax.tree.map(lambda a: a.astype(jnp.bfloat16) if a.dtype == jnp.float32 else a, value)


def angle_table(count, left, right):
    product = left[:, None] * right[None, :] % count
    angle = product.astype(jnp.float32) * (2.0 * math.pi / count)
    return (jnp.cos(angle), jnp.sin(angle))


def contract(pattern, table, values):
    return jnp.einsum(pattern, table, values, precision=highest_precision)


def rotate(pattern, cos_table, sin_table, real_part, imag_part, turning):
    out_real = contract(pattern, cos_table, real_part) - turning * contract(
        pattern, sin_table, imag_part
    )
    out_imag = contract(pattern, cos_table, imag_part) + turning * contract(
        pattern, sin_table, real_part
    )
    return (out_real, out_imag)


def frequency_order(groups):
    return jnp.arange(2 * groups, dtype=jnp.int32)


def shards(q_proj, k_proj, v_proj, feat_filter, long_filter, skip_bias, norm_gain):
    rows = q_proj.shape[0]
    taps = feat_filter.shape[1]
    groups = lax.axis_size("seq")
    stacked = jnp.stack([q_proj, k_proj, v_proj])
    previous = shifted(stacked[:, rows - (taps - 1) :, :], "seq", 1)
    extended = jnp.concatenate([previous, stacked], axis=1)
    featured = jnp.zeros(stacked.shape, jnp.float32)
    for offset in range(taps):
        window = extended[:, taps - 1 - offset : taps - 1 - offset + rows, :]
        featured = featured + feat_filter[:, offset, None, :] * window.astype(jnp.float32)
    query = featured[0]
    gated = featured[1] * featured[2]
    device = lax.axis_index("seq")
    per_device = rows // groups
    length = 2 * rows * groups
    order = frequency_order(groups)
    blocks = jnp.arange(groups, dtype=jnp.int32)
    within = jnp.arange(rows, dtype=jnp.int32)
    local_rows = device * per_device + jnp.arange(per_device, dtype=jnp.int32)
    slots = lax.dynamic_slice_in_dim(order, 2 * device, 2)
    cos_a, sin_a = angle_table(2 * groups, order, blocks)
    cos_w, sin_w = angle_table(length, order, local_rows)
    cos_b, sin_b = angle_table(rows, within, within)
    cos_v, sin_v = angle_table(length, slots, within)
    cos_i, sin_i = angle_table(2 * groups, blocks, order)
    signals = jnp.stack([gated, long_filter])[:, None]
    pieces = lax.all_to_all(
        signals.astype(jnp.bfloat16), "seq", split_axis=2, concat_axis=1, tiled=True
    ).astype(signals.dtype)
    real_part = contract("ka,xabc->xkbc", cos_a, pieces)
    imag_part = -contract("ka,xabc->xkbc", sin_a, pieces)
    cosine = cos_w[:, :, None]
    sine = sin_w[:, :, None]
    real_part, imag_part = (
        real_part * cosine + imag_part * sine,
        imag_part * cosine - real_part * sine,
    )
    spread = jnp.stack([real_part, imag_part], axis=1)
    pieces = lax.all_to_all(
        for_sending(spread), "seq", split_axis=2, concat_axis=3, tiled=True
    ).astype(spread.dtype)
    real_part, imag_part = rotate("kb,xsbc->xskc", cos_b, sin_b, pieces[:, 0], pieces[:, 1], -1.0)
    prod_real = real_part[0] * real_part[1] - imag_part[0] * imag_part[1]
    prod_imag = real_part[0] * imag_part[1] + imag_part[0] * real_part[1]
    real_part = prod_real
    imag_part = prod_imag
    real_part, imag_part = rotate("bk,skc->sbc", cos_b, sin_b, real_part, imag_part, 1.0)
    cosine = cos_v[:, :, None]
    sine = sin_v[:, :, None]
    spectra = jnp.stack(
        [real_part * cosine - imag_part * sine, imag_part * cosine + real_part * sine]
    )
    pieces = lax.all_to_all(
        for_sending(spectra), "seq", split_axis=2, concat_axis=1, tiled=True
    ).astype(spectra.dtype)
    summed = contract("ak,kbc->abc", cos_i, pieces[0]) - contract("ak,kbc->abc", sin_i, pieces[1])
    returned = summed / length
    long_conv = lax.all_to_all(
        for_sending(returned), "seq", split_axis=0, concat_axis=1, tiled=True
    ).astype(returned.dtype)[0]
    mixed = query * (long_conv + skip_bias * gated)
    squares = lax.psum(jnp.sum(mixed * mixed, axis=1), "ch")
    scale = lax.rsqrt(squares / D + 1e-05)
    normed = (mixed * scale[:, None] * norm_gain).astype(jnp.bfloat16)
    return (mixed.astype(jnp.bfloat16), normed)


def mixer_kernel(
    n, inner,
    q_hbm, k_hbm, v_hbm, filter_hbm, f_full_hbm, f_real_hbm, g_full_hbm, g_real_hbm,
    feat_hbm, skip_hbm, gain_hbm,
    mixed_ref, normed_ref,
    feat_ref, skip_ref, gain_ref, q_ref, k_ref, v_ref, filter_ref, f_full, f_real, g_full, g_real,
    tails, send_f, send_g, send_y, recv_f, recv_g, recv_y, query, gated, sums, other_sums,
    y_full, y_real, low_full, low_real, h_full, h_real,
    local_sem, tail_send, tail_recv, f_send, f_recv, g_send, g_recv, y_send, y_recv, sum_sem,
):
    me = lax.axis_index("seq")
    core = lax.axis_index("ch")
    other = 1 - core
    rows = q_ref.shape[0]
    after = lax.rem(me + 1, n)

    def at(block):
        return pl.ds(pl.multiple_of(block * rows, rows), rows)

    def lanes(block):
        return pl.ds(pl.multiple_of(block * LANES, LANES), LANES)

    def partner(j):
        offset = n // 2 + ((j + 1) // 2) * (2 * (j % 2) - 1)
        return lax.rem(me + offset, n)

    loads = [
        pltpu.make_async_copy(source, target, local_sem.at[i])
        for i, (source, target) in enumerate([
            (filter_hbm, filter_ref), (k_hbm, k_ref), (v_hbm, v_ref), (q_hbm, q_ref),
            (feat_hbm, feat_ref), (skip_hbm, skip_ref), (gain_hbm, gain_ref),
            (f_real_hbm, f_real), (f_full_hbm, f_full), (g_real_hbm, g_real), (g_full_hbm, g_full),
        ])
    ]
    for load in loads[:7]:
        load.start()

    barrier = pltpu.get_barrier_semaphore()

    def greet(j, carry):
        pl.semaphore_signal(
            barrier, inc=1, device_id=(partner(j), core), device_id_type=MESH
        )
        return carry

    lax.fori_loop(0, n - 1, greet, 0)
    pl.semaphore_signal(barrier, inc=1, device_id=(me, other), device_id_type=MESH)

    loads[0].wait()

    def narrow(j, carry):
        send_f[at(j), :] = filter_ref[:, lanes(j)].astype(jnp.bfloat16)
        return carry

    lax.fori_loop(0, n, narrow, 0)
    recv_f[at(me), :] = send_f[at(me), :]
    for load in loads[1:7]:
        load.wait()
    pl.semaphore_wait(barrier, n)

    def tail_copy(i, ref):
        return pltpu.make_async_remote_copy(
            src_ref=ref.at[pl.ds(rows - 16, 16), :],
            dst_ref=tails.at[i],
            send_sem=tail_send.at[i],
            recv_sem=tail_recv.at[i],
            device_id=(after, core),
            device_id_type=MESH,
        )

    tail_copies = [tail_copy(i, ref) for i, ref in enumerate((k_ref, v_ref, q_ref))]
    for copy in tail_copies:
        copy.start()

    def exchange(source, target, send_sem, recv_sem):
        def to(peer):
            return pltpu.make_async_remote_copy(
                src_ref=source.at[at(peer), :],
                dst_ref=target.at[at(me), :],
                send_sem=send_sem.at[peer],
                recv_sem=recv_sem.at[me],
                device_id=(peer, core),
                device_id_type=MESH,
            )

        def come(peer):
            return pltpu.make_async_remote_copy(
                src_ref=source.at[at(peer), :],
                dst_ref=target.at[at(peer), :],
                send_sem=send_sem.at[peer],
                recv_sem=recv_sem.at[peer],
                device_id=(peer, core),
                device_id_type=MESH,
            )

        def start(j, carry):
            to(partner(j)).start()
            return carry

        def arrive(j, carry):
            come(partner(n - 2 - j)).wait_recv()
            return carry

        def leave(j, carry):
            to(partner(j)).wait_send()
            return carry

        return (
            lambda: lax.fori_loop(0, n - 1, start, 0),
            lambda: lax.fori_loop(0, n - 1, arrive, 0),
            lambda: lax.fori_loop(0, n - 1, leave, 0),
            come,
        )

    start_f, arrive_f, leave_f, _ = exchange(send_f, recv_f, f_send, f_recv)
    start_g, arrive_g, leave_g, _ = exchange(send_g, recv_g, g_send, g_recv)
    start_y, _, leave_y, come_y = exchange(send_y, recv_y, y_send, y_recv)
    start_f()
    for load in loads[7:]:
        load.start()

    first = me == 0

    def featured(stream, tail, ref, j):
        columns = lanes(j)
        before = tails[tail, :, columns].astype(jnp.float32)
        before = jnp.where(first, 0.0, before)
        window = jnp.concatenate([before, ref[:, columns].astype(jnp.float32)])
        total = feat_ref[stream, 0:1, columns] * window[16:]
        for tap in (1, 2):
            moved = pltpu.roll(window, tap, 0)[16:]
            total = total + feat_ref[stream, tap : tap + 1, columns] * moved
        return total

    for copy in tail_copies[:2]:
        copy.wait()

    def gate(j, carry):
        value = featured(1, 0, k_ref, j) * featured(2, 1, v_ref, j)
        gated[at(j), :] = value
        send_g[at(j), :] = value.astype(jnp.bfloat16)
        return carry

    lax.fori_loop(0, n, gate, 0)
    start_g()
    recv_g[at(me), :] = send_g[at(me), :]
    tail_copies[2].wait()

    def ask(j, carry):
        query[at(j), :] = featured(0, 2, q_ref, j)
        return carry

    lax.fori_loop(0, n, ask, 0)

    def block_of(ref):
        def load(block, start):
            where = pl.ds(pl.multiple_of(block * inner + start, CHUNK), CHUNK)
            return ref[where, :].astype(jnp.float32)

        return load

    def store(block, start, value):
        send_y[pl.ds(pl.multiple_of(block * inner + start, CHUNK), CHUNK), :] = value

    for load in loads[7:]:
        load.wait()
    arrive_f()
    spread_blocks(inner, block_of(recv_f), y_full, y_real, (low_full, low_real))
    filter_spectrum(f_full, f_real, y_full, y_real, low_full, low_real, h_full, h_real)
    arrive_g()
    spread_blocks(inner, block_of(recv_g), y_full, y_real)
    filtered(inner, f_full, f_real, g_full, g_real, y_full, y_real, h_full, h_real)
    gather_blocks(inner, h_full, h_real, store)
    start_y()
    recv_y[at(me), :] = send_y[at(me), :]

    def mix(block):
        conv = recv_y[at(block), :].astype(jnp.float32)
        mixed = query[at(block), :] * (conv + skip_ref[:, lanes(block)] * gated[at(block), :])
        query[at(block), :] = mixed
        mixed_ref[:, lanes(block)] = mixed.astype(jnp.bfloat16)
        return mixed * mixed

    def mix_next(j, carry):
        block = partner(n - 2 - j)
        come_y(block).wait_recv()
        return carry + mix(block)

    sums[...] = lax.fori_loop(0, n - 1, mix_next, mix(me))
    sum_copy = pltpu.make_async_remote_copy(
        src_ref=sums,
        dst_ref=other_sums,
        send_sem=sum_sem.at[0],
        recv_sem=sum_sem.at[1],
        device_id=(me, other),
        device_id_type=MESH,
    )
    sum_copy.start()
    leave_f()
    leave_g()
    leave_y()
    sum_copy.wait()
    total = jnp.sum(sums[...] + other_sums[...], axis=1, keepdims=True)
    scale = lax.rsqrt(total / D + 1e-05)

    def norm(j, carry):
        value = query[at(j), :] * scale * gain_ref[:, lanes(j)]
        normed_ref[:, lanes(j)] = value.astype(jnp.bfloat16)
        return carry

    lax.fori_loop(0, n, norm, 0)


def channel_shards(q_proj, k_proj, v_proj, feat_filter, long_filter, skip_bias, norm_gain):
    rows, channels = q_proj.shape
    n = lax.axis_size("seq")
    seq = rows * n
    inner = seq // HALF
    tables = [jnp.asarray(t) for t in dft_tables(seq)]
    narrow, wide = jnp.bfloat16, jnp.float32
    scratch = [pltpu.VMEM(feat_filter.shape, wide), pltpu.VMEM((1, channels), wide)]
    scratch += [pltpu.VMEM((1, channels), wide)]
    scratch += [pltpu.VMEM((rows, channels), narrow)] * 3 + [pltpu.VMEM((rows, channels), wide)]
    scratch += [pltpu.VMEM(t.shape, narrow) for t in tables]
    scratch += [pltpu.VMEM((3, 16, channels), narrow)]
    scratch += [pltpu.VMEM((seq, LANES), narrow)] * 6
    scratch += [pltpu.VMEM((seq, LANES), wide)] * 2
    scratch += [pltpu.VMEM((rows, LANES), wide)] * 2
    scratch += spectrum_scratch(inner)
    scratch += [pltpu.SemaphoreType.DMA((11,))]
    scratch += [pltpu.SemaphoreType.DMA((3,))] * 2
    scratch += [pltpu.SemaphoreType.DMA((n,))] * 6
    scratch += [pltpu.SemaphoreType.DMA((2,))]
    away = pl.BlockSpec(memory_space=pltpu.HBM)
    whole = pl.BlockSpec(memory_space=pltpu.VMEM)
    out = jax.ShapeDtypeStruct((rows, channels), narrow)
    operands = [q_proj, k_proj, v_proj, long_filter, *tables, feat_filter]
    operands += [skip_bias.reshape(1, -1), norm_gain.reshape(1, -1)]
    return tuple(pl.pallas_call(
        functools.partial(mixer_kernel, n, inner),
        out_shape=(out, out),
        in_specs=[away] * 11,
        out_specs=(whole, whole),
        scratch_shapes=scratch,
        compiler_params=pltpu.CompilerParams(
            collective_id=0, has_side_effects=True, vmem_limit_bytes=VMEM_BYTES
        ),
    )(*[pltpu.with_memory_space_constraint(a, pltpu.HBM) for a in operands]))


def solution(mesh):
    def layer(*arrays):
        rows, channels = arrays[0].shape
        n = mesh.shape["seq"]
        seq = rows * n
        whole_lanes = channels == LANES * n and n % 4 == 0 and rows % 64 == 0 and mesh.shape["ch"] == 2
        if whole_lanes and seq % (2 * HALF * CHUNK) == 0 and seq <= 2048:
            return channel_shards(*arrays)
        return shards(*arrays)

    return jax.shard_map(
        layer,
        mesh=mesh,
        in_specs=(
            P("seq", "ch"),
            P("seq", "ch"),
            P("seq", "ch"),
            P(None, None, "ch"),
            P("seq", "ch"),
            P("ch"),
            P("ch"),
        ),
        out_specs=(P("seq", "ch"), P("seq", "ch")),
        check_vma=False,
    )
```
